256 devices in a mesh: box: 32 (over y, z), depth: 8 (over x, core).
Axes of the slice: x: 4, y: 4, z: 8, core: 2. Of those that a mesh axis runs over, the one named last changes fastest.
Arguments:
- state: float32 [5, 64, 256, 384], P(None, 'depth', 'box')
- velocity: float32 [3, 64, 256, 384], P(None, 'depth', 'box'), may hold values from -6 to 6
- bins: int32 [64, 256, 384], P('depth', 'box'), may hold values from 0 to 4095, as said below
Outputs:
- new_state: float32 [5, 64, 256, 384], P(None, 'depth', 'box')
- potential: float32 [64, 256, 384], P('depth', 'box')
- base_profile: float32 [5, 4096], replicated
The draws below stay inside these ranges and needn't reach their ends.
Inputs may be any that keep to these rules, and one draw needn't show every extreme that they name: `bins`: bins grow with the squared distance of a cell from a centre cell inside the grid, which has bin 0.
All inputs are finite; a program needn't handle non-finite values. Where the reference program divides by a largest or mean magnitude, that divisor is 1e-20 or more.
Results may differ from the reference program's by a relative error of at most 0.0003.
Values sent between devices are 32-bit elements; how exact they have to be, the bound alone decides.
No kernel may reach another device: no remote copies, remote signals or barrier semaphores. Data moves between devices by JAX's collectives and lax.ppermute only.
A program may use at most 64 MiB of HBM per device.

```python
import jax
import jax.numpy as jnp

NBINS = 4096
NFIELDS = 5
ITERS = 4
NX = 64
NY = 256
NZ = 384


def draw_state(key, part):
    key = jax.random.fold_in(key, 11)
    slope_key, noise_key = jax.random.split(key)
    slopes = jax.random.uniform(slope_key, (NFIELDS, 3), jnp.float32, -3.0, 3.0)
    coord_x = 2.0 * jnp.arange(NX, dtype=jnp.float32) / NX - 1.0
    coord_y = 2.0 * jnp.arange(NY, dtype=jnp.float32) / NY - 1.0
    coord_z = 2.0 * jnp.arange(NZ, dtype=jnp.float32) / NZ - 1.0
    ramp = slopes[:, 0, None, None, None] * coord_x[None, :, None, None]
    ramp = ramp + slopes[:, 1, None, None, None] * coord_y[None, None, :, None]
    ramp = ramp + slopes[:, 2, None, None, None] * coord_z[None, None, None, :]
    noise = jax.random.normal(noise_key, (NFIELDS, NX, NY, NZ), jnp.float32)
    return (ramp + noise).astype(jnp.float32)


def draw_bins(key, part):
    key = jax.random.fold_in(key, 23)
    offsets = jax.random.randint(key, (3,), -2, 3)
    dist_x = jnp.arange(NX, dtype=jnp.int32) - (NX // 2 + offsets[0])
    dist_y = jnp.arange(NY, dtype=jnp.int32) - (NY // 2 + offsets[1])
    dist_z = jnp.arange(NZ, dtype=jnp.int32) - (NZ // 2 + offsets[2])
    radius_sq = dist_x[:, None, None] ** 2 + dist_y[None, :, None] ** 2 + dist_z[None, None, :] ** 2
    largest = jnp.max(radius_sq) // 8
    return (radius_sq // 8 * (NBINS - 1) // largest).astype(jnp.int32)


def level_of(key, shape, cuts, low, high):
    factor_of, own = 1.0, jax.random.fold_in(key, 6)
    for dim, parts in cuts:
        steps = jnp.exp(jax.random.uniform(jax.random.fold_in(own, dim), (parts,), jnp.float32, low / len(cuts), high / len(cuts)))
        factor_of = factor_of * jnp.repeat(steps, shape[dim] // parts).reshape([-1 if axis == dim else 1 for axis in range(len(shape))])
    return factor_of


def scatter_about(stream_key, dims, spread, limit, cuts=(), held_as=jnp.bfloat16):
    entries = jax.random.normal(stream_key, dims, jnp.float32) * spread
    if len(cuts) > 0:
        entries = level_of(stream_key, dims, cuts, -0.22, 0.18) * entries
    return jnp.clip(entries, min=-limit, max=limit).astype(held_as)


def setup_inputs(seed: int = 0) -> dict:
    seeds = jax.random.split(jax.random.key(seed), 4)
    state = draw_state(jax.random.fold_in(seeds[3], 71), 0)
    velocity = scatter_about(seeds[1], (3, NX, NY, NZ), 1.0, 6.0, ((1, 8), (2, 32)), jnp.float32)
    bins = draw_bins(jax.random.fold_in(seeds[3], 71), 0)
    return dict(state=state, velocity=velocity, bins=bins)


COURANT = 0.8
OMEGA_RELAX = 0.8
KAPPA_SHIFT = 0.1
RHS_WEIGHTS = (1.0, 0.5, -0.5, 0.25, 0.75)


def bin_average(fields, flat_bins, counts):
    columns = fields.reshape(fields.shape[0], -1)
    sums = jax.vmap(lambda column: jax.ops.segment_sum(column, flat_bins, num_segments=NBINS))(columns)
    return sums / jnp.maximum(counts, 1.0)


def upwind(padded, velocity, time_step):
    center = padded[:, 1:-1, 1:-1, 1:-1]
    lowers = (padded[:, :-2, 1:-1, 1:-1], padded[:, 1:-1, :-2, 1:-1], padded[:, 1:-1, 1:-1, :-2])
    uppers = (padded[:, 2:, 1:-1, 1:-1], padded[:, 1:-1, 2:, 1:-1], padded[:, 1:-1, 1:-1, 2:])
    change = jnp.zeros_like(center)
    for axis_index in range(3):
        comp_speed = velocity[axis_index][None]
        change = change + jnp.maximum(comp_speed, 0.0) * (center - lowers[axis_index]) + jnp.minimum(comp_speed, 0.0) * (uppers[axis_index] - center)
    return center - time_step * change


def relax(padded, source):
    center = padded[1:-1, 1:-1, 1:-1]
    beside = padded[2:, 1:-1, 1:-1] + padded[:-2, 1:-1, 1:-1]
    beside = beside + padded[1:-1, 2:, 1:-1] + padded[1:-1, :-2, 1:-1]
    beside = beside + padded[1:-1, 1:-1, 2:] + padded[1:-1, 1:-1, :-2]
    diagonal = 6.0 + KAPPA_SHIFT
    return center + OMEGA_RELAX * (source - (diagonal * center - beside)) / diagonal


def projection_source(new_state, lifted):
    source = jnp.zeros_like(new_state[0])
    for field_index in range(len(RHS_WEIGHTS)):
        source = source + RHS_WEIGHTS[field_index] * (new_state[field_index] - lifted[field_index])
    return source


def reference(state, velocity, bins):
    flat_bins = bins.reshape(-1)
    counts = jax.ops.segment_sum(jnp.ones(flat_bins.shape, jnp.float32), flat_bins, num_segments=NBINS)
    first = bin_average(state, flat_bins, counts)
    top_speed = jnp.max(jnp.sum(jnp.abs(velocity), axis=0))
    time_step = COURANT / (top_speed + 1.0)
    first_lift = jnp.take(first, bins, axis=1)
    perturb = state - first_lift
    padded = jnp.pad(perturb, ((0, 0), (1, 1), (1, 1), (1, 1)))
    new_state = first_lift + upwind(padded, velocity, time_step)
    second = bin_average(new_state, flat_bins, counts)
    source = projection_source(new_state, jnp.take(second, bins, axis=1))
    potential = jnp.zeros_like(source)
    for sweep_index in range(ITERS):
        potential = relax(jnp.pad(potential, 1), source)
    return new_state, potential, second
```

```python
import jax
import jax.numpy as jnp
from jax import lax
from jax.experimental import pallas as pl
from jax.experimental.pallas import tpu as pltpu
from jax.sharding import PartitionSpec as P

NBINS = 4096
COURANT = 0.8
OMEGA_RELAX = 0.8
DIAGONAL = 6.1
WEIGHTS = (1.0, 0.5, -0.5, 0.25, 0.75)
NF = 5
X, Y, Z = 8, 8, 384
TILES = NBINS // 128
REACH = 3
F32, BF16 = jnp.float32, jnp.bfloat16
VMEM_BYTES = 48 * 1024 * 1024


def pieces_of(values):
    upper = values.astype(BF16).astype(F32)
    rest = values - upper
    middle = rest.astype(BF16).astype(F32)
    return upper, middle, rest - middle


def lo_table(lo_row):
    wide = jnp.broadcast_to(lo_row, (16, Z)).astype(BF16)
    row = lax.broadcasted_iota(jnp.int32, (16, Z), 0).astype(F32).astype(BF16)
    one, zero = jnp.ones((16, Z), BF16), jnp.zeros((16, Z), BF16)
    return jnp.concatenate([jnp.where(wide == row + jnp.asarray(16 * k, BF16), one, zero) for k in range(16)], axis=0)


def hi_rows(hi_row, rows16):
    wide = jnp.broadcast_to(hi_row, (16, Z)).astype(BF16)
    zero = jnp.zeros((16, Z), BF16)
    return jnp.concatenate([jnp.where(wide == jnp.asarray(k, BF16), rows16, zero) for k in range(16)], axis=0)


def put_rows(rows, p, values):
    for j in range(3):
        rows[j, pl.ds(p, Y, stride=16), :] = values[:, j * 128 : (j + 1) * 128]


def get_rows(rows, y):
    return jnp.concatenate([rows[j, pl.ds(16 * y, 16), :].astype(BF16) for j in range(3)], axis=1)


def get_field(lifted, x, f):
    return jnp.concatenate([lifted[x, j, pl.ds(f, Y, stride=8), :] for j in range(3)], axis=1)


def add_bins(acc, rows, hi, lo, x):
    left, right = [], []
    for y in range(Y):
        left.append(hi_rows(hi[x, pl.ds(y, 1), :], get_rows(rows, y)))
        right.append(lo_table(lo[x, pl.ds(y, 1), :]))
    acc[...] += lax.dot_general(
        jnp.concatenate(left, 1), jnp.concatenate(right, 1), (((1,), (1,)), ((), ())), preferred_element_type=F32
    )


def put_sums(out, acc, extra):
    for k in range(16):
        s = acc[pl.ds(16 * k, 16), :]
        tile = jnp.concatenate([s[0:5] + s[5:10] + s[10:15], s[15:16], extra], axis=0)
        out[2 * k] = tile[:, :128]
        out[2 * k + 1] = tile[:, 128:]


def split_bins(bins, hi, lo):
    b = bins[...]
    hi[...] = lax.shift_right_logical(b, 8).astype(F32)
    lo[...] = (b & 255).astype(F32)


def sums_kernel(state, velocity, bins, out, hi, lo, rows, acc):
    split_bins(bins, hi, lo)
    acc[...] = jnp.zeros_like(acc)
    put_rows(rows, 15, jnp.ones((Y, Z), F32))

    def step(x, carry):
        for f in range(NF):
            for i, piece in enumerate(pieces_of(state[f, x])):
                put_rows(rows, NF * i + f, piece)
        add_bins(acc, rows, hi, lo, x)
        return carry

    lax.fori_loop(0, X, step, 0)
    top = jnp.max(jnp.abs(velocity[0]) + jnp.abs(velocity[1]) + jnp.abs(velocity[2]))
    put_sums(out, acc, jnp.full((2, 256), top, F32))


def digits(b):
    h = jnp.floor(b * (1.0 / 256.0))
    return h, b - 256.0 * h


def lift_row(table, hi_row, lo_row):
    found = lax.dot_general(table, lo_table(lo_row), (((1,), (0,)), ((), ())), preferred_element_type=F32)
    wide = jnp.broadcast_to(hi_row, (16, Z))
    acc = jnp.zeros((16, Z), F32)
    for k in range(16):
        acc = jnp.where(wide == float(k), found[16 * k : 16 * k + 16], acc)
    total = acc[0:5] + acc[5:10] + acc[10:15]
    return jnp.concatenate([total, jnp.zeros((3, Z), F32)], axis=0)


def step_kernel(
    first, state, velocity, bins, ylo, yhi, xlo, xhi, new_state, q_out, out, hi, lo, face_hi, face_lo, table, lifted, p, rows, acc
):
    for k in range(16):
        pair = jnp.concatenate([first[2 * k], first[2 * k + 1]], axis=1)
        u, m, l = pieces_of(pair)
        block = jnp.concatenate([u[0:5], m[0:5], l[0:5], jnp.zeros((1, 256), F32)], axis=0)
        table[pl.ds(16 * k, 16), :] = block.astype(BF16)
    tab = table[...]
    time_step = COURANT / (1.0 + jnp.max(first[0, 6:7, :]))
    split_bins(bins, hi, lo)
    for s, (ref, near) in enumerate(((xlo, 7), (xhi, 5))):
        face_hi[s], face_lo[s] = digits(ref[near] - 1.0)

    def lift_x(x, carry):
        for y in range(Y):
            eight = lift_row(tab, hi[x, pl.ds(y, 1), :], lo[x, pl.ds(y, 1), :])
            for j in range(3):
                lifted[x, j, pl.ds(8 * y, 8), :] = eight[:, 128 * j : 128 * j + 128]
        for f in range(NF):
            p[f, x + 1, pl.ds(8, 8), :] = state[f, x] - get_field(lifted, x, f)
        for ref, at, near in ((ylo, 7, 7), (yhi, 16, 5)):
            h, l = digits(ref[x, near : near + 1, :] - 1.0)
            eight = ref[x] - lift_row(tab, h, l)
            for f in range(NF):
                p[f, x + 1, at : at + 1, :] = eight[f : f + 1]
        return carry

    lax.fori_loop(0, X, lift_x, 0)
    for s, (ref, at) in enumerate(((xlo, 0), (xhi, X + 1))):
        for y in range(Y):
            eight = lift_row(tab, face_hi[s, y : y + 1, :], face_lo[s, y : y + 1, :])
            for j in range(3):
                lifted[X, j, pl.ds(8 * y, 8), :] = eight[:, 128 * j : 128 * j + 128]
        for f in range(NF):
            p[f, at, pl.ds(8, 8), :] = ref[f] - get_field(lifted, X, f)

    acc[...] = jnp.zeros_like(acc)
    lane = lax.broadcasted_iota(jnp.int32, (Y, Z), 1)
    put_rows(rows, 15, jnp.zeros((Y, Z), F32))

    def advect(x, carry):
        v = [velocity[d, x] for d in range(3)]
        up = [jnp.maximum(c, 0.0) for c in v]
        down = [jnp.minimum(c, 0.0) for c in v]
        q = jnp.zeros((Y, Z), F32)
        for f in range(NF):
            c = p[f, x + 1, pl.ds(8, 8), :]
            before = jnp.where(lane == 0, 0.0, pltpu.roll(c, 1, 1))
            after = jnp.where(lane == Z - 1, 0.0, pltpu.roll(c, Z - 1, 1))
            change = up[0] * (c - p[f, x, pl.ds(8, 8), :]) + down[0] * (p[f, x + 2, pl.ds(8, 8), :] - c)
            change += up[1] * (c - p[f, x + 1, pl.ds(7, 8), :]) + down[1] * (p[f, x + 1, pl.ds(9, 8), :] - c)
            change += up[2] * (c - before) + down[2] * (after - c)
            moved = c - time_step * change
            new_state[f, x] = get_field(lifted, x, f) + moved
            q += WEIGHTS[f] * moved
            for i, piece in enumerate(pieces_of(moved)):
                put_rows(rows, NF * i + f, piece)
        q_out[x] = q
        add_bins(acc, rows, hi, lo, x)
        return carry

    lax.fori_loop(0, X, advect, 0)
    put_sums(out, acc, jnp.zeros((2, 256), F32))


def relax_kernel(
    second, first, q, qylo, qyhi, qxlo, qxhi, bins, ylo, yhi, xlo, xhi, potential, profile, table, digit, src, pot
):
    total = jnp.zeros((TILES, 128), F32)
    for t in range(TILES):
        profile[:, 128 * t : 128 * t + 128] = (first[t] + second[t])[0:NF]
    for f in range(NF):
        total += WEIGHTS[f] * second[:, f, :]
    cols = jnp.concatenate([total[:, 0:64], total[:, 64:128]], axis=0)
    upper = cols.astype(BF16).astype(F32)
    table[...] = jnp.concatenate([upper, cols - upper], axis=1).astype(BF16)
    tab = table[...]
    src[...] = jnp.zeros_like(src)
    digit[...] = jnp.full(digit.shape, -1.0, F32)
    src[pl.ds(3, 8), 8:16, :] = q[...]
    src[pl.ds(3, 8), 5:8, :] = qylo[...]
    src[pl.ds(3, 8), 16:19, :] = qyhi[...]
    digit[pl.ds(3, 8), 8:16, :] = bins[...].astype(F32)
    digit[pl.ds(3, 8), 5:8, :] = ylo[:, 5:8, :] - 1.0
    digit[pl.ds(3, 8), 16:19, :] = yhi[:, 5:8, :] - 1.0
    for at, qref, bref in ((0, qxlo, xlo), (11, qxhi, xhi)):
        for dst, ref, base, less in ((src, qref, 0, 0.0), (digit, bref, NF, 1.0)):
            dst[pl.ds(at, 3), 8:16, :] = ref[pl.ds(base, 3)] - less
            dst[pl.ds(at, 3), 5:8, :] = ref[pl.ds(base + 3, 3), 0:3, :] - less
            dst[pl.ds(at, 3), 16:19, :] = ref[pl.ds(base + 3, 3), 3:6, :] - less
    row = lax.broadcasted_iota(jnp.int32, (64, Z), 0).astype(F32)
    row16 = lax.broadcasted_iota(jnp.int32, (16, Z), 0).astype(F32).astype(BF16)
    one, zero = jnp.ones((16, Z), BF16), jnp.zeros((16, Z), BF16)

    def lift_x(x, carry):
        for y in range(5, 19):
            b = digit[x, y : y + 1, :]
            h = jnp.floor(b * (1.0 / 64.0))
            l = jnp.broadcast_to(b - 64.0 * h, (16, Z)).astype(BF16)
            g = jnp.floor(h * 0.5)
            h = jnp.where(b < 0.0, -1.0, g + 32.0 * (h - 2.0 * g))
            t = jnp.concatenate([jnp.where(l == row16 + jnp.asarray(16 * k, BF16), one, zero) for k in range(4)], axis=0)
            o = lax.dot_general(tab, jnp.concatenate([t, t], axis=0), (((1,), (0,)), ((), ())), preferred_element_type=F32)
            o = jnp.where(jnp.broadcast_to(h, (64, Z)) == row, o, 0.0)
            src[x, y : y + 1, :] = src[x, y : y + 1, :] - jnp.sum(o, axis=0, keepdims=True)
        return carry

    lax.fori_loop(0, 14, lift_x, 0)
    lane = lax.broadcasted_iota(jnp.int32, (24, Z), 1)

    def start(x, carry):
        pot[0, x] = src[x] * (OMEGA_RELAX / DIAGONAL)
        return carry

    lax.fori_loop(0, 14, start, 0)
    for s in range(1, 4):
        now, later = (s + 1) % 2, s % 2

        def sweep(x, carry):
            c = pot[now, x]
            near = pot[now, x - 1] + pot[now, x + 1]
            near += pltpu.roll(c, 1, 0) + pltpu.roll(c, 23, 0)
            near += jnp.where(lane == 0, 0.0, pltpu.roll(c, 1, 1)) + jnp.where(lane == Z - 1, 0.0, pltpu.roll(c, Z - 1, 1))
            new = c + OMEGA_RELAX * (src[x] - (DIAGONAL * c - near)) / DIAGONAL
            if s < 3:
                pot[later, x] = jnp.where(digit[x] < 0.0, 0.0, new)
            else:
                potential[x - 3] = new[8:16]
            return carry

        lax.fori_loop(s, 14 - s, sweep, 0)


def call(kernel, out_shape, scratch, *args):
    return pl.pallas_call(
        kernel,
        out_shape=out_shape,
        scratch_shapes=[pltpu.VMEM(shape, dtype) for shape, dtype in scratch],
        compiler_params=pltpu.CompilerParams(vmem_limit_bytes=VMEM_BYTES),
    )(*args)


def f32_like(*shape):
    return jax.ShapeDtypeStruct(shape, F32)


def from_below(face, axis):
    count = lax.axis_size(axis)
    return lax.ppermute(face, axis, [(i, i + 1) for i in range(count - 1)])


def from_above(face, axis):
    count = lax.axis_size(axis)
    return lax.ppermute(face, axis, [(i + 1, i) for i in range(count - 1)])


def beside(below, above, part):
    gap = jnp.zeros((REACH, 2, Z), F32)
    return jnp.concatenate([below[part], above[part], gap], axis=1)


def merge(tiles):
    total = jnp.sum(tiles, axis=0)
    top = jnp.max(tiles, axis=0)
    row = lax.broadcasted_iota(jnp.int32, total.shape, 1)
    return jnp.where(row == 6, top, total)


def own_share(tiles):
    depth, box = lax.axis_size("depth"), lax.axis_size("box")
    share = tiles.reshape(depth, TILES // depth, 8, 128)
    share = merge(lax.all_to_all(share, "depth", 0, 0, tiled=True))
    copies = jnp.broadcast_to(share[None], (box,) + share.shape)
    return merge(lax.all_to_all(copies, "box", 0, 0, tiled=True))


def spread(share):
    depth = lax.axis_size("depth")
    copies = jnp.broadcast_to(share[None], (depth,) + share.shape)
    return lax.all_to_all(copies, "depth", 0, 0, tiled=True).reshape(TILES, 8, 128)


def per_device(state, velocity, bins):
    shifted = bins.astype(F32) + 1.0
    ylo = from_below(jnp.concatenate([jnp.swapaxes(state[:, :, Y - 1], 0, 1), shifted[:, Y - REACH :]], axis=1), "box")
    yhi = from_above(jnp.concatenate([jnp.swapaxes(state[:, :, 0], 0, 1), shifted[:, :REACH]], axis=1), "box")
    low, high = slice(0, REACH), slice(X - REACH, X)
    xfaces = []
    for part, edge in ((high, X - 1), (low, 0)):
        corners = beside(ylo[:, NF:], yhi[:, NF:], part)
        xfaces.append(jnp.concatenate([state[:, edge], shifted[part], corners], axis=0))
    xlo = from_below(xfaces[0], "depth")
    xhi = from_above(xfaces[1], "depth")
    tiles = call(
        sums_kernel,
        f32_like(TILES, 8, 128),
        [((X, Y, Z), F32), ((X, Y, Z), F32), ((3, Y * 16, 128), F32), ((256, 256), F32)],
        state, velocity, bins,
    )
    share = own_share(tiles)
    counts = jnp.maximum(share[:, 5:6], 1.0)
    row = lax.broadcasted_iota(jnp.int32, share.shape, 1)
    first = spread(jnp.where(row < NF, share / counts, share))
    new_state, q, tiles = call(
        step_kernel,
        (f32_like(NF, X, Y, Z), f32_like(X, Y, Z), f32_like(TILES, 8, 128)),
        [
            ((X, Y, Z), F32), ((X, Y, Z), F32), ((2, Y, Z), F32), ((2, Y, Z), F32), ((256, 256), BF16),
            ((X + 1, 3, 64, 128), F32), ((NF, X + 2, 24, Z), F32), ((3, Y * 16, 128), F32), ((256, 256), F32),
        ],
        first, state, velocity, bins, ylo, yhi, xlo, xhi,
    )
    qylo = from_below(q[:, Y - REACH :], "box")
    qyhi = from_above(q[:, :REACH], "box")
    qxlo = from_below(jnp.concatenate([q[high], beside(qylo, qyhi, high)], axis=0), "depth")
    qxhi = from_above(jnp.concatenate([q[low], beside(qylo, qyhi, low)], axis=0), "depth")
    second = spread(own_share(tiles) / counts)
    potential, profile = call(
        relax_kernel,
        (f32_like(X, Y, Z), f32_like(NF, NBINS)),
        [((64, 128), BF16), ((14, 24, Z), F32), ((14, 24, Z), F32), ((2, 14, 24, Z), F32)],
        second, first, q, qylo, qyhi, qxlo, qxhi, bins, ylo, yhi, xlo, xhi,
    )
    return (new_state, potential, profile)


def solution(mesh):
    return jax.shard_map(
        per_device,
        mesh=mesh,
        in_specs=(
            P(None, "depth", "box", None),
            P(None, "depth", "box", None),
            P("depth", "box", None),
        ),
        out_specs=(P(None, "depth", "box", None), P("depth", "box", None), P()),
        check_vma=False,
    )
```

```python
import math

import jax
import jax.numpy as jnp
import numpy as np
from jax import lax
from jax.experimental import pallas as pl
from jax.experimental.pallas import tpu as pltpu
from jax.sharding import PartitionSpec as P

NBINS = 4096
COURANT = 0.8
OMEGA_RELAX = 0.8
DIAGONAL = 6.1
WEIGHTS = (1.0, 0.5, -0.5, 0.25, 0.75)
NF = 5
X, Y, Z = 8, 8, 384
TILES = NBINS // 128
SW, BN, VE, CSW, CBN, CVE, PLANES = 5, 9, 13, 22, 25, 28, 34
TALL = 24
MEMBERS = 16
F32, BF16 = jnp.float32, jnp.bfloat16


def pieces_of(values):
    upper = values.astype(BF16).astype(F32)
    rest = values - upper
    middle = rest.astype(BF16).astype(F32)
    return upper, middle, rest - middle


def lo_table(lo_row):
    wide = jnp.broadcast_to(lo_row, (16, Z)).astype(BF16)
    row = lax.broadcasted_iota(jnp.int32, (16, Z), 0).astype(F32).astype(BF16)
    one, zero = jnp.ones((16, Z), BF16), jnp.zeros((16, Z), BF16)
    return jnp.concatenate([jnp.where(wide == row + jnp.asarray(16 * k, BF16), one, zero) for k in range(16)], axis=0)


def hi_rows(hi_row, rows16):
    wide = jnp.broadcast_to(hi_row, (16, Z)).astype(BF16)
    zero = jnp.zeros((16, Z), BF16)
    return jnp.concatenate([jnp.where(wide == jnp.asarray(k, BF16), rows16, zero) for k in range(16)], axis=0)


def put_rows(rows, p, values):
    for j in range(3):
        rows[j, pl.ds(p, Y, stride=16), :] = values[:, j * 128 : (j + 1) * 128]


def get_rows(rows, y):
    return jnp.concatenate([rows[j, pl.ds(16 * y, 16), :].astype(BF16) for j in range(3)], axis=1)


def get_field(lifted, x, f):
    return jnp.concatenate([lifted[x, j, pl.ds(f, Y, stride=8), :] for j in range(3)], axis=1)


def add_bins(acc, rows, hi, lo, x):
    left, right = [], []
    for y in range(Y):
        left.append(hi_rows(hi[x, pl.ds(y, 1), :], get_rows(rows, y)))
        right.append(lo_table(lo[x, pl.ds(y, 1), :]))
    acc[...] += lax.dot_general(
        jnp.concatenate(left, 1), jnp.concatenate(right, 1), (((1,), (1,)), ((), ())), preferred_element_type=F32
    )


def put_sums(out, acc, extra):
    for k in range(16):
        s = acc[pl.ds(16 * k, 16), :]
        tile = jnp.concatenate([s[0:5] + s[5:10] + s[10:15], s[15:16], extra], axis=0)
        out[2 * k] = tile[:, :128]
        out[2 * k + 1] = tile[:, 128:]


def split_bins(bins, hi, lo):
    b = bins[...]
    hi[...] = lax.shift_right_logical(b, 8).astype(F32)
    lo[...] = (b & 255).astype(F32)


def sums_kernel(
    state_in, velocity_in, bins_in, to_above, to_below, weighted, shifted, out, hi, lo, rows, acc, state, velocity, bins, sems, more_sems
):
    bins_copy = pltpu.make_async_copy(bins_in, bins, more_sems.at[0])
    bins_copy.start()
    copies = [
        [pltpu.make_async_copy(state_in.at[f, pl.ds(4 * h, 4)], state.at[f, pl.ds(4 * h, 4)], sems.at[h, f]) for f in range(NF)]
        for h in range(2)
    ]
    speed_copies = [pltpu.make_async_copy(velocity_in.at[d], velocity.at[d], more_sems.at[1 + d]) for d in range(3)]
    for copy in copies[0] + speed_copies + copies[1]:
        copy.start()
    acc[...] = jnp.zeros_like(acc)
    put_rows(rows, 15, jnp.ones((Y, Z), F32))
    bins_copy.wait()
    split_bins(bins, hi, lo)

    def step(x, top):
        s = [state[f, x] for f in range(NF)]
        w = WEIGHTS[0] * s[0]
        for f in range(NF):
            for i, piece in enumerate(pieces_of(s[f])):
                put_rows(rows, NF * i + f, piece)
            if f > 0:
                w += WEIGHTS[f] * s[f]
        add_bins(acc, rows, hi, lo, x)
        weighted[x] = w
        b = bins[x].astype(F32) + 1.0
        shifted[x] = b
        v = [velocity[d, x] for d in range(3)]
        for face, near, four, three in ((to_above, Y - 1, Y - 4, Y - 3), (to_below, 0, 0, 0)):
            parts = [c[near : near + 1] for c in s] + [w[four : four + 4], b[four : four + 4]]
            parts += [c[three : three + 3] for c in v] + [jnp.zeros((2, Z), F32)]
            face[x] = jnp.concatenate(parts, axis=0)
        return jnp.maximum(top, jnp.abs(v[0]) + jnp.abs(v[1]) + jnp.abs(v[2]))

    top = jnp.zeros((Y, Z), F32)
    for h in range(2):
        for copy in copies[h] + (speed_copies if h == 0 else []):
            copy.wait()
        top = lax.fori_loop(4 * h, 4 * h + 4, step, top)
    put_sums(out, acc, jnp.full((2, 256), jnp.max(top), F32))


def pack_x_kernel(state, velocity, weighted, shifted, ylo, yhi, to_above, to_below, corners, sems):
    copies = []
    for side, (out, near, four, three) in enumerate(((to_above, X - 1, X - 4, X - 3), (to_below, 0, 0, 0))):
        parts = [(state.at[:, near], 0, NF), (weighted.at[pl.ds(four, 4)], SW, 4), (shifted.at[pl.ds(four, 4)], BN, 4)]
        parts += [(velocity.at[d, pl.ds(three, 3)], VE + 3 * d, 3) for d in range(3)]
        for i, (src, at, n) in enumerate(parts):
            copies.append(pltpu.make_async_copy(src, out.at[pl.ds(at, n)], sems.at[side, i]))
    for copy in copies:
        copy.start()
    gap = jnp.zeros((1, Z), F32)
    for side, (out, three, two) in enumerate(((to_above, X - 3, X - 2), (to_below, 0, 0))):
        for i in range(3):
            x = three + i
            for at, row in ((CSW, SW), (CBN, BN)):
                corners[side, at - CSW + i] = jnp.concatenate([ylo[x, row : row + 4], yhi[x, row : row + 4]], axis=0)
        for i in range(2):
            x = two + i
            for d in range(3):
                row = VE + 3 * d
                corners[side, CVE - CSW + 2 * d + i] = jnp.concatenate(
                    [ylo[x, row : row + 3], gap, yhi[x, row : row + 3], gap], axis=0
                )
        copies.append(pltpu.make_async_copy(corners.at[side], out.at[pl.ds(CSW, PLANES - CSW)], sems.at[side, 6]))
        copies[-1].start()
    for copy in copies:
        copy.wait()


def lift_row(table, hi_row, lo_row):
    found = lax.dot_general(table, lo_table(lo_row), (((1,), (0,)), ((), ())), preferred_element_type=F32)
    wide = jnp.broadcast_to(hi_row, (16, Z))
    acc = jnp.zeros((16, Z), F32)
    for k in range(16):
        acc = jnp.where(wide == float(k), found[16 * k : 16 * k + 16], acc)
    total = acc[0:5] + acc[5:10] + acc[10:15]
    return jnp.concatenate([total, jnp.zeros((3, Z), F32)], axis=0)


def lift_five(first, b):
    index = b.astype(jnp.int32)
    parts = [[] for f in range(NF)]
    for j in range(3):
        cut = index[:, 128 * j : 128 * j + 128]
        tile, lane = lax.shift_right_arithmetic(cut, 7), cut & 127
        found = [jnp.zeros((8, 128), F32)] * NF
        for t in range(TILES):
            here = tile == t
            for f in range(NF):
                row = jnp.broadcast_to(first[t, f : f + 1, :], (8, 128))
                found[f] = jnp.where(here, jnp.take_along_axis(row, lane, axis=1), found[f])
        for f in range(NF):
            parts[f].append(found[f])
    return [jnp.concatenate(part, axis=1) for part in parts]


def step_kernel(
    first, state, velocity, bins, ylo, yhi, xlo, xhi, new_state_out, near_out, out,
    hi, lo, face_bins, face_lift, table, lifted, p, rows, acc, new_state, near_p, sems
):
    for k in range(16):
        pair = jnp.concatenate([first[2 * k], first[2 * k + 1]], axis=1)
        u, m, l = pieces_of(pair)
        block = jnp.concatenate([u[0:5], m[0:5], l[0:5], jnp.zeros((1, 256), F32)], axis=0)
        table[pl.ds(16 * k, 16), :] = block.astype(BF16)
    tab = table[...]
    time_step = COURANT / (1.0 + jnp.max(first[0, 6:7, :]))
    split_bins(bins, hi, lo)
    for x in range(X):
        face_bins[0, x : x + 1, :] = ylo[x, BN + 3 : BN + 4, :] - 1.0
        face_bins[1, x : x + 1, :] = yhi[x, BN : BN + 1, :] - 1.0
    face_bins[2] = xlo[BN + 3] - 1.0
    face_bins[3] = xhi[BN] - 1.0

    def lift_some(i, carry):
        for k in range(2):
            x = 2 * i + k
            for y in range(Y):
                eight = lift_row(tab, hi[x, pl.ds(y, 1), :], lo[x, pl.ds(y, 1), :])
                for j in range(3):
                    lifted[x, j, pl.ds(8 * y, 8), :] = eight[:, 128 * j : 128 * j + 128]
        for f, value in enumerate(lift_five(first, face_bins[i])):
            face_lift[i, f] = value
        for k in range(2):
            x = 2 * i + k
            for f in range(NF):
                p[f, x + 1, pl.ds(8, 8), :] = state[f, x] - get_field(lifted, x, f)
        return carry

    lax.fori_loop(0, 4, lift_some, 0)
    for f in range(NF):
        p[f, 0, pl.ds(8, 8), :] = xlo[f] - face_lift[2, f]
        p[f, X + 1, pl.ds(8, 8), :] = xhi[f] - face_lift[3, f]
        for x in range(X):
            p[f, x + 1, 7:8, :] = ylo[x, f : f + 1, :] - face_lift[0, f, x : x + 1, :]
            p[f, x + 1, 16:17, :] = yhi[x, f : f + 1, :] - face_lift[1, f, x : x + 1, :]

    acc[...] = jnp.zeros_like(acc)
    lane = lax.broadcasted_iota(jnp.int32, (Y, Z), 1)
    put_rows(rows, 15, jnp.zeros((Y, Z), F32))

    def advect(x, carry):
        v = [velocity[d, x] for d in range(3)]
        up = [jnp.maximum(c, 0.0) for c in v]
        down = [jnp.minimum(c, 0.0) for c in v]
        for f in range(NF):
            c = p[f, x + 1, pl.ds(8, 8), :]
            before = jnp.where(lane == 0, 0.0, pltpu.roll(c, 1, 1))
            after = jnp.where(lane == Z - 1, 0.0, pltpu.roll(c, Z - 1, 1))
            change = up[0] * (c - p[f, x, pl.ds(8, 8), :]) + down[0] * (p[f, x + 2, pl.ds(8, 8), :] - c)
            change += up[1] * (c - p[f, x + 1, pl.ds(7, 8), :]) + down[1] * (p[f, x + 1, pl.ds(9, 8), :] - c)
            change += up[2] * (c - before) + down[2] * (after - c)
            moved = c - time_step * change
            new_state[f, x] = get_field(lifted, x, f) + moved
            for i, piece in enumerate(pieces_of(moved)):
                put_rows(rows, NF * i + f, piece)
        state_copy(x).start()
        add_bins(acc, rows, hi, lo, x)
        return carry

    def state_copy(x):
        return pltpu.make_async_copy(new_state.at[:, x], new_state_out.at[:, x], sems.at[x])


    def gather_p(x, carry):
        total = WEIGHTS[0] * p[0, x]
        for f in range(1, NF):
            total += WEIGHTS[f] * p[f, x]
        near_p[x] = total
        return carry

    lax.fori_loop(0, X + 2, gather_p, 0)
    near_copy = pltpu.make_async_copy(near_p, near_out, sems.at[X])
    near_copy.start()
    lax.fori_loop(0, X, advect, 0)
    put_sums(out, acc, jnp.zeros((2, 256), F32))
    for x in range(X):
        state_copy(x).wait()
    near_copy.wait()


def weighted_rows(tiles):
    total = jnp.zeros((TILES, 128), F32)
    for f in range(NF):
        total += WEIGHTS[f] * tiles[:, f, :]
    return total


def row_table(total, pieces):
    return jnp.concatenate(pieces_of(total)[:pieces], axis=0).astype(BF16)


def lift_one(tab, b):
    high = jnp.floor(b * (1.0 / 128.0))
    low = b - 128.0 * high
    row = lax.broadcasted_iota(jnp.int32, (TILES, Z), 0).astype(F32)
    row16 = lax.broadcasted_iota(jnp.int32, (16, Z), 0).astype(F32).astype(BF16)
    one, zero = jnp.ones((16, Z), BF16), jnp.zeros((16, Z), BF16)
    wide = jnp.broadcast_to(low, (16, Z)).astype(BF16)
    t = jnp.concatenate([jnp.where(wide == row16 + jnp.asarray(16 * k, BF16), one, zero) for k in range(8)], axis=0)
    found = lax.dot_general(tab, t, (((1,), (0,)), ((), ())), preferred_element_type=F32)
    total = found[0:TILES]
    for i in range(1, tab.shape[0] // TILES):
        total += found[TILES * i : TILES * i + TILES]
    return jnp.sum(jnp.where(jnp.broadcast_to(high, (TILES, Z)) == row, total, 0.0), axis=0, keepdims=True)


def lift_eight(table, b):
    index = b.astype(jnp.int32)
    parts = []
    for j in range(3):
        cut = index[:, 128 * j : 128 * j + 128]
        tile, lane = lax.shift_right_arithmetic(cut, 7), cut & 127
        found = jnp.zeros((8, 128), F32)
        for t in range(TILES):
            row = jnp.broadcast_to(table[t : t + 1, :], (8, 128))
            found = jnp.where(tile == t, jnp.take_along_axis(row, lane, axis=1), found)
        parts.append(found)
    return jnp.concatenate(parts, axis=1)


def reach_rows(far):
    near = {0: range(7, 17), 1: range(8, 16)}
    return {d: [y for y in range(8 - far + d, 16 + far - d) if y not in near.get(d, ())] for d in range(far + 1)}


def ring_kernel(
    first, near_p, shifted, velocity, ylo, yhi, xlo, xhi, q_out, bins_out, p, q, high, v, faces, flat, sems, v_sems, out_sems
):
    blocks = [
        (near_p, p.at[pl.ds(3, 10)]),
        (xlo.at[pl.ds(SW, 3)], p.at[pl.ds(0, 3), pl.ds(8, 8)]),
        (xhi.at[pl.ds(SW + 1, 3)], p.at[pl.ds(13, 3), pl.ds(8, 8)]),
        (shifted, high.at[pl.ds(4, 8), pl.ds(8, 8)]),
        (xlo.at[pl.ds(BN, 4)], high.at[pl.ds(0, 4), pl.ds(8, 8)]),
        (xhi.at[pl.ds(BN, 4)], high.at[pl.ds(12, 4), pl.ds(8, 8)]),
        (ylo, faces.at[0, pl.ds(0, 8)]),
        (yhi, faces.at[1, pl.ds(0, 8)]),
        (xlo.at[pl.ds(CSW, 12)], faces.at[2, pl.ds(0, 12), pl.ds(0, 8)]),
        (xhi.at[pl.ds(CSW, 12)], faces.at[3, pl.ds(0, 12), pl.ds(0, 8)]),
    ]
    early = [pltpu.make_async_copy(src, dst, sems.at[i]) for i, (src, dst) in enumerate(blocks)]
    late = []
    for d in range(3):
        parts = ((velocity.at[d], 3, 8), (xlo.at[pl.ds(VE + 3 * d, 3)], 0, 3), (xhi.at[pl.ds(VE + 3 * d, 3)], 11, 3))
        for i, (src, at, n) in enumerate(parts):
            late.append(pltpu.make_async_copy(src, v.at[d, pl.ds(at, n), pl.ds(8, 8)], v_sems.at[d, i]))
    for copy in early + late:
        copy.start()
    flat[...] = weighted_rows(first)
    tab = row_table(flat[...], 3)
    for copy in early:
        copy.wait()
    below, above, left, right = (faces.at[i] for i in range(4))
    p[pl.ds(4, 8), 4:7, :] = below[0:8, SW : SW + 3, :]
    p[pl.ds(4, 8), 17:20, :] = above[0:8, SW + 1 : SW + 4, :]
    high[pl.ds(4, 8), 4:8, :] = below[0:8, BN : BN + 4, :]
    high[pl.ds(4, 8), 16:20, :] = above[0:8, BN : BN + 4, :]
    for dst, corner in ((p, 0), (high, CBN - CSW)):
        for ref, at in ((left, 1), (right, 12)):
            dst[pl.ds(at, 3), 4:8, :] = ref[pl.ds(corner, 3), 0:4, :]
            dst[pl.ds(at, 3), 16:20, :] = ref[pl.ds(corner, 3), 4:8, :]
    bins_copy = pltpu.make_async_copy(high, bins_out, out_sems.at[0])
    bins_copy.start()
    rows = reach_rows(4)

    def lift_x(x, rows, block):
        if block:
            p[x, 8:16, :] = p[x, 8:16, :] - lift_eight(flat, high[x, 8:16, :] - 1.0)
        for y in rows:
            p[x, y : y + 1, :] = p[x, y : y + 1, :] - lift_one(tab, high[x, y : y + 1, :] - 1.0)

    def lift_sides(side, carry):
        for d in range(2, 5):
            lift_x((4 - d) + side * (7 + 2 * d), [y for y in rows[d] if not 8 <= y < 16], True)
        lift_x(3 + side * 9, rows[1], False)
        for i in range(4):
            lift_x(4 + 4 * side + i, rows[0], False)
        return carry

    lax.fori_loop(0, 2, lift_sides, 0)
    for copy in late:
        copy.wait()
    for d in range(3):
        row, corner = VE + 3 * d, CVE - CSW + 2 * d
        v[d, pl.ds(3, 8), 5:8, :] = below[0:8, row : row + 3, :]
        v[d, pl.ds(3, 8), 16:19, :] = above[0:8, row : row + 3, :]
        for ref, at in ((left, 1), (right, 11)):
            v[d, pl.ds(at, 2), 5:8, :] = ref[pl.ds(corner, 2), 0:3, :]
            v[d, pl.ds(at, 2), 16:19, :] = ref[pl.ds(corner, 2), 4:7, :]
    time_step = COURANT / (1.0 + jnp.max(first[0, 6:7, :]))
    lane = lax.broadcasted_iota(jnp.int32, (TALL, Z), 1)

    def step(x, carry):
        c = p[x + 1]
        sides = (
            (p[x], p[x + 2]),
            (pltpu.roll(c, 1, 0), pltpu.roll(c, TALL - 1, 0)),
            (jnp.where(lane == 0, 0.0, pltpu.roll(c, 1, 1)), jnp.where(lane == Z - 1, 0.0, pltpu.roll(c, Z - 1, 1))),
        )
        change = jnp.zeros((TALL, Z), F32)
        for d, (before, after) in enumerate(sides):
            change += jnp.maximum(v[d, x], 0.0) * (c - before) + jnp.minimum(v[d, x], 0.0) * (after - c)
        q[x] = c - time_step * change
        return carry

    lax.fori_loop(0, 14, step, 0)
    q_copy = pltpu.make_async_copy(q, q_out, out_sems.at[1])
    q_copy.start()
    q_copy.wait()
    bins_copy.wait()


def relax_kernel(second, first, q_in, bins_in, potential, profile, src, high, pot, flat, sems):
    halves = []
    for h in range(2):
        at = pl.ds(3 + 4 * h, 4)
        bins_at = pl.ds(4 + 4 * h, 4)
        halves.append((q_in.at[at], src.at[at], bins_in.at[bins_at], high.at[bins_at]))
    for at, n in ((0, 3), (11, 3)):
        bins_at = pl.ds(at + 1, n)
        halves.append((q_in.at[pl.ds(at, n)], src.at[pl.ds(at, n)], bins_in.at[bins_at], high.at[bins_at]))
    copies = [
        [pltpu.make_async_copy(parts[2 * i], parts[2 * i + 1], sems.at[h, i]) for i in range(2)] for h, parts in enumerate(halves)
    ]
    for pair in copies:
        for copy in pair:
            copy.start()
    flat[...] = weighted_rows(second)
    tab = row_table(flat[...], 2)
    for t in range(TILES):
        profile[:, 128 * t : 128 * t + 128] = (first[t] + second[t])[0:NF]

    def lift_x(x, rows, block):
        if block:
            src[x, 8:16, :] = src[x, 8:16, :] - lift_eight(flat, high[x + 1, 8:16, :] - 1.0)
        for y in rows:
            src[x, y : y + 1, :] = src[x, y : y + 1, :] - lift_one(tab, high[x + 1, y : y + 1, :] - 1.0)
        scaled = src[x] * (OMEGA_RELAX / DIAGONAL)
        src[x] = scaled
        pot[0, x] = scaled

    def lift_sides(side, carry):
        for d in range(1, 4):
            rows = [y for y in range(5 + d, 19 - d) if d == 3 or not 8 <= y < 16]
            lift_x((3 - d) + side * (7 + 2 * d), rows, d < 3)
        return carry

    for h in range(2):
        for copy in copies[h]:
            copy.wait()
        lax.fori_loop(3 + 4 * h, 7 + 4 * h, lambda x, c: (lift_x(x, (5, 6, 7, 16, 17, 18), True), c)[1], 0)
    for pair in copies[2:]:
        for copy in pair:
            copy.wait()
    lax.fori_loop(0, 2, lift_sides, 0)
    lane = lax.broadcasted_iota(jnp.int32, (TALL, Z), 1)
    for s in range(1, 4):
        now, later = (s + 1) % 2, s % 2

        def sweep(x, carry):
            c = pot[now, x]
            near = pot[now, x - 1] + pot[now, x + 1]
            near += pltpu.roll(c, 1, 0) + pltpu.roll(c, TALL - 1, 0)
            near += jnp.where(lane == 0, 0.0, pltpu.roll(c, 1, 1)) + jnp.where(lane == Z - 1, 0.0, pltpu.roll(c, Z - 1, 1))
            new = (1.0 - OMEGA_RELAX) * c + (src[x] + (OMEGA_RELAX / DIAGONAL) * near)
            if s < 3:
                pot[later, x] = jnp.where(high[x + 1] < 0.5, 0.0, new)
            else:
                potential[x - 3] = new[8:16]
            return carry

        lax.fori_loop(s, 14 - s, sweep, 0)


def f32_like(*shape):
    return jax.ShapeDtypeStruct(shape, F32)


def call(kernel, plan, *args):
    micros, out_shape, scratch, more = plan
    more = dict(more)
    limit = more.pop("megabytes") * 1024 * 1024
    return pl.pallas_call(
        kernel,
        out_shape=out_shape,
        cost_estimate=pl.CostEstimate(flops=micros * 1_000_000_000, bytes_accessed=0, transcendentals=0),
        scratch_shapes=[pltpu.VMEM(*part) if isinstance(part, tuple) else part for part in scratch],
        compiler_params=pltpu.CompilerParams(vmem_limit_bytes=limit),
        **more,
    )(*args)


def from_below(face, axis):
    count = lax.axis_size(axis)
    return lax.ppermute(face, axis, [(i, i + 1) for i in range(count - 1)])


def from_above(face, axis):
    count = lax.axis_size(axis)
    return lax.ppermute(face, axis, [(i + 1, i) for i in range(count - 1)])


def added(tiles):
    total, top = tiles[0], tiles[0]
    for i in range(1, MEMBERS):
        total, top = total + tiles[i], jnp.maximum(top, tiles[i])
    return jnp.where(lax.broadcasted_iota(jnp.int32, total.shape, 1) == 6, top, total)


def merge_kernel(tiles, share, copies):
    total = added(tiles)
    share[...] = total
    for i in range(MEMBERS):
        copies[i] = total


def divide_kernel(tiles, counts, share, copies):
    total = added(tiles)
    cells = total if counts is None else counts
    row = lax.broadcasted_iota(jnp.int32, total.shape, 1)
    mean = jnp.where(row < NF, total / jnp.maximum(cells[:, 5:6, :], 1.0), total)
    share[...] = total
    for i in range(MEMBERS):
        copies[i] = mean


def divide_own_kernel(tiles, share, copies):
    divide_kernel(tiles, None, share, copies)


def groups_of(varied):
    sizes = (4, 8, 4, 2)
    fixed = [d for d in range(4) if d not in varied]
    places = np.arange(256).reshape(sizes).transpose(fixed + list(varied))
    return places.reshape(-1, math.prod(sizes[d] for d in varied)).tolist()


SHARE_GROUPS = groups_of((0, 2))
OTHER_GROUPS = groups_of((1, 3))
def swap(parts, groups):
    return lax.all_to_all(parts, ("box", "depth"), 0, 0, axis_index_groups=groups, tiled=True)


def in_members(tiles):
    return tiles.reshape(MEMBERS, TILES // MEMBERS, 8, 128)


VISIBLE = pl.BlockSpec(memory_space=pltpu.VMEM)
REMOTE = pl.BlockSpec(memory_space=pl.ANY)
SUMS = (
    7,
    (f32_like(X, TALL, Z), f32_like(X, TALL, Z), f32_like(X, Y, Z), f32_like(X, Y, Z), f32_like(TILES, 8, 128)),
    [
        ((X, Y, Z), F32), ((X, Y, Z), F32), ((3, Y * 16, 128), F32), ((256, 256), F32),
        ((NF, X, Y, Z), F32), ((3, X, Y, Z), F32), ((X, Y, Z), jnp.int32),
        pltpu.SemaphoreType.DMA((2, NF)), pltpu.SemaphoreType.DMA((4,)),
    ],
    dict(in_specs=[REMOTE] * 3, megabytes=58),
)
PACK_X = (
    2,
    (f32_like(PLANES, Y, Z), f32_like(PLANES, Y, Z)),
    [((2, PLANES - CSW, Y, Z), F32), pltpu.SemaphoreType.DMA((2, 7))],
    dict(in_specs=[REMOTE] * 4 + [VISIBLE] * 2, out_specs=(REMOTE, REMOTE), megabytes=20),
)
STEP = (
    14,
    (f32_like(NF, X, Y, Z), f32_like(X + 2, TALL, Z), f32_like(TILES, 8, 128)),
    [
        ((X, Y, Z), F32), ((X, Y, Z), F32), ((4, Y, Z), F32), ((4, NF, Y, Z), F32), ((256, 256), BF16),
        ((X, 3, 64, 128), F32), ((NF, X + 2, TALL, Z), F32), ((3, Y * 16, 128), F32), ((256, 256), F32),
        ((NF, X, Y, Z), F32), ((X + 2, TALL, Z), F32), pltpu.SemaphoreType.DMA((X + 1,)),
    ],
    dict(out_specs=(REMOTE, REMOTE, VISIBLE), megabytes=24),
)
RING = (
    8,
    (f32_like(14, TALL, Z), f32_like(16, TALL, Z)),
    [
        ((16, TALL, Z), F32), ((14, TALL, Z), F32), ((16, TALL, Z), F32), ((3, 14, TALL, Z), F32), ((4, 12, TALL, Z), F32), ((TILES, 128), F32),
        pltpu.SemaphoreType.DMA((10,)), pltpu.SemaphoreType.DMA((3, 3)), pltpu.SemaphoreType.DMA((2,)),
    ],
    dict(in_specs=[VISIBLE] + [REMOTE] * 7, out_specs=(REMOTE, REMOTE), megabytes=58),
)
RELAX = (
    9,
    (f32_like(X, Y, Z), f32_like(NF, NBINS)),
    [((14, TALL, Z), F32), ((16, TALL, Z), F32), ((2, 14, TALL, Z), F32), ((TILES, 128), F32), pltpu.SemaphoreType.DMA((4, 2))],
    dict(in_specs=[VISIBLE] * 2 + [REMOTE] * 2, megabytes=58),
)


MERGE = (1, (f32_like(2, 8, 128), f32_like(MEMBERS, 2, 8, 128)), [], dict(megabytes=20))


def per_device(state, velocity, bins):
    to_above, to_below, weighted, shifted, tiles = call(sums_kernel, SUMS, state, velocity, bins)
    ylo = from_below(to_above, "box")
    yhi = from_above(to_below, "box")
    to_above, to_below = call(pack_x_kernel, PACK_X, state, velocity, weighted, shifted, ylo, yhi)
    xlo = from_below(to_above, "depth")
    xhi = from_above(to_below, "depth")
    share, copies = call(merge_kernel, MERGE, swap(in_members(tiles), SHARE_GROUPS))
    share, copies = call(divide_own_kernel, MERGE, swap(copies, OTHER_GROUPS))
    first = swap(copies, SHARE_GROUPS).reshape(TILES, 8, 128)
    new_state, near_p, tiles = call(step_kernel, STEP, first, state, velocity, bins, ylo, yhi, xlo, xhi)
    q, wide_bins = call(ring_kernel, RING, first, near_p, shifted, velocity, ylo, yhi, xlo, xhi)
    part, copies = call(merge_kernel, MERGE, swap(in_members(tiles), SHARE_GROUPS))
    copies, q, wide_bins = lax.optimization_barrier((copies, q, wide_bins))
    part, copies = call(divide_kernel, MERGE, swap(copies, OTHER_GROUPS), share)
    second = swap(copies, SHARE_GROUPS).reshape(TILES, 8, 128)
    potential, profile = call(relax_kernel, RELAX, second, first, q, wide_bins)
    return (new_state, potential, profile)


def solution(mesh):
    return jax.shard_map(
        per_device,
        mesh=mesh,
        in_specs=(
            P(None, "depth", "box", None),
            P(None, "depth", "box", None),
            P("depth", "box", None),
        ),
        out_specs=(P(None, "depth", "box", None), P("depth", "box", None), P()),
        check_vma=False,
    )
```

```python
import functools
import math

import jax
import jax.numpy as jnp
import numpy as np
from jax import lax
from jax.experimental import pallas as pl
from jax.experimental.pallas import tpu as pltpu
from jax.sharding import PartitionSpec as P

NBINS = 4096
COURANT = 0.8
OMEGA_RELAX = 0.8
DIAGONAL = 6.1
WEIGHTS = (1.0, 0.5, -0.5, 0.25, 0.75)
NF = 5
X, Y, Z = 8, 8, 384
TILES = NBINS // 128
SW, BN, VE, CSW, CBN, CVE, PLANES = 5, 9, 13, 22, 25, 28, 34
TALL = 24
MEMBERS = 16
F32, BF16 = jnp.float32, jnp.bfloat16


def pieces_of(values):
    upper = values.astype(BF16).astype(F32)
    rest = values - upper
    middle = rest.astype(BF16).astype(F32)
    return upper, middle, rest - middle


def lo_table(lo_row):
    wide = jnp.broadcast_to(lo_row, (16, Z)).astype(BF16)
    row = lax.broadcasted_iota(jnp.int32, (16, Z), 0).astype(F32).astype(BF16)
    one, zero = jnp.ones((16, Z), BF16), jnp.zeros((16, Z), BF16)
    return jnp.concatenate([jnp.where(wide == row + jnp.asarray(16 * k, BF16), one, zero) for k in range(16)], axis=0)


def hi_rows(hi_row, rows16):
    wide = jnp.broadcast_to(hi_row, (16, Z)).astype(BF16)
    zero = jnp.zeros((16, Z), BF16)
    return jnp.concatenate([jnp.where(wide == jnp.asarray(k, BF16), rows16, zero) for k in range(16)], axis=0)


def put_rows(rows, p, values):
    for j in range(3):
        rows[j, pl.ds(p, Y, stride=16), :] = values[:, j * 128 : (j + 1) * 128]


def get_rows(rows, y):
    return jnp.concatenate([rows[j, pl.ds(16 * y, 16), :].astype(BF16) for j in range(3)], axis=1)


def get_field(lifted, x, f):
    return jnp.concatenate([lifted[x, j, pl.ds(f, Y, stride=8), :] for j in range(3)], axis=1)


def add_bins(acc, rows, hi, lo, x):
    left, right = [], []
    for y in range(Y):
        left.append(hi_rows(hi[x, pl.ds(y, 1), :], get_rows(rows, y)))
        right.append(lo_table(lo[x, pl.ds(y, 1), :]))
    acc[...] += lax.dot_general(
        jnp.concatenate(left, 1), jnp.concatenate(right, 1), (((1,), (1,)), ((), ())), preferred_element_type=F32
    )


def put_sums(out, acc, extra):
    for k in range(16):
        s = acc[pl.ds(16 * k, 16), :]
        tile = jnp.concatenate([s[0:5] + s[5:10] + s[10:15], s[15:16], extra], axis=0)
        out[2 * k] = tile[:, :128]
        out[2 * k + 1] = tile[:, 128:]


def split_bins(bins, hi, lo):
    b = bins[...]
    hi[...] = lax.shift_right_logical(b, 8).astype(F32)
    lo[...] = (b & 255).astype(F32)


def is_odd(axis):
    return lax.rem(lax.axis_index(axis), 2) == 1


def start_by(odd, make, even_place, odd_place):
    @pl.when(jnp.logical_not(odd))
    def _():
        for copy in make(even_place, odd_place):
            copy.start()

    @pl.when(odd)
    def _():
        for copy in make(odd_place, even_place):
            copy.start()


def sums_kernel(
    state_in, velocity_in, bins_in, mate_out, next_out, weighted_out, shifted_out, out,
    hi, lo, rows, acc, state, velocity, bins, to_above, to_below, weighted, shifted, sems, out_sems
):
    bins_copy = pltpu.make_async_copy(bins_in, bins, sems.at[4, 0])
    bins_copy.start()

    def arrive(h):
        at = pl.ds(2 * h, 2)
        return [
            pltpu.make_async_copy(state_in.at[:, at], state.at[:, at], sems.at[h, 0]),
            pltpu.make_async_copy(velocity_in.at[:, at], velocity.at[:, at], sems.at[h, 1]),
        ]

    def leave(h, above_out, below_out):
        at = pl.ds(4 * h, 4)
        pairs = ((to_above, above_out), (to_below, below_out), (weighted, weighted_out), (shifted, shifted_out))
        return [pltpu.make_async_copy(src.at[at], dst.at[at], out_sems.at[h, i]) for i, (src, dst) in enumerate(pairs)]

    for h in range(4):
        for copy in arrive(h):
            copy.start()
    acc[...] = jnp.zeros_like(acc)
    put_rows(rows, 15, jnp.ones((Y, Z), F32))
    bins_copy.wait()
    split_bins(bins, hi, lo)
    shifted[...] = bins[...].astype(F32) + 1.0

    def step(x, top):
        s = [state[f, x] for f in range(NF)]
        w = WEIGHTS[0] * s[0]
        for f in range(NF):
            for i, piece in enumerate(pieces_of(s[f])):
                put_rows(rows, NF * i + f, piece)
            if f > 0:
                w += WEIGHTS[f] * s[f]
        add_bins(acc, rows, hi, lo, x)
        weighted[x] = w
        b = shifted[x]
        v = [velocity[d, x] for d in range(3)]
        for face, near, four, three in ((to_above, Y - 1, Y - 4, Y - 3), (to_below, 0, 0, 0)):
            parts = [c[near : near + 1] for c in s] + [w[four : four + 4], b[four : four + 4]]
            parts += [c[three : three + 3] for c in v] + [jnp.zeros((2, Z), F32)]
            face[x] = jnp.concatenate(parts, axis=0)
        return jnp.maximum(top, jnp.abs(v[0]) + jnp.abs(v[1]) + jnp.abs(v[2]))

    top = jnp.zeros((Y, Z), F32)
    for h in range(4):
        for copy in arrive(h):
            copy.wait()
        top = lax.fori_loop(2 * h, 2 * h + 2, step, top)
        if h % 2 == 1:
            start_by(is_odd("box"), functools.partial(leave, h // 2), mate_out, next_out)
    put_sums(out, acc, jnp.full((2, 256), jnp.max(top), F32))
    for h in range(2):
        for copy in leave(h, mate_out, next_out):
            copy.wait()


def pack_x_kernel(state, velocity, weighted, shifted, ymate, ynext, mate_out, next_out, corners, sems):
    def fill(to_above, to_below):
        copies = []
        for side, (out, near, four, three) in enumerate(((to_above, X - 1, X - 4, X - 3), (to_below, 0, 0, 0))):
            parts = [(state.at[:, near], 0, NF), (weighted.at[pl.ds(four, 4)], SW, 4), (shifted.at[pl.ds(four, 4)], BN, 4)]
            parts += [(velocity.at[d, pl.ds(three, 3)], VE + 3 * d, 3) for d in range(3)]
            for i, (src, at, n) in enumerate(parts):
                copies.append(pltpu.make_async_copy(src, out.at[pl.ds(at, n)], sems.at[side, i]))
        return copies

    def fill_corners(to_above, to_below):
        return [
            pltpu.make_async_copy(corners.at[side], out.at[pl.ds(CSW, PLANES - CSW)], sems.at[side, 6])
            for side, out in enumerate((to_above, to_below))
        ]

    start_by(is_odd("depth"), fill, mate_out, next_out)
    odd = is_odd("box")
    gap = jnp.zeros((1, Z), F32)
    for side, (three, two) in enumerate(((X - 3, X - 2), (0, 0))):
        for x in range(three, three + 3):
            ylo, yhi = jnp.where(odd, ymate[x], ynext[x]), jnp.where(odd, ynext[x], ymate[x])
            for at, row in ((CSW, SW), (CBN, BN)):
                corners[side, at - CSW + x - three] = jnp.concatenate([ylo[row : row + 4], yhi[row : row + 4]], axis=0)
            if 0 <= x - two < 2:
                for d in range(3):
                    row = VE + 3 * d
                    corners[side, CVE - CSW + 2 * d + x - two] = jnp.concatenate(
                        [ylo[row : row + 3], gap, yhi[row : row + 3], gap], axis=0
                    )
    start_by(is_odd("depth"), fill_corners, mate_out, next_out)
    for copy in fill(mate_out, next_out) + fill_corners(mate_out, next_out):
        copy.wait()


def lift_row(table, hi_row, lo_row):
    found = lax.dot_general(table, lo_table(lo_row), (((1,), (0,)), ((), ())), preferred_element_type=F32)
    wide = jnp.broadcast_to(hi_row, (16, Z))
    acc = jnp.zeros((16, Z), F32)
    for k in range(16):
        acc = jnp.where(wide == float(k), found[16 * k : 16 * k + 16], acc)
    total = acc[0:5] + acc[5:10] + acc[10:15]
    return jnp.concatenate([total, jnp.zeros((3, Z), F32)], axis=0)


def lift_five(first, b):
    index = b.astype(jnp.int32)
    parts = [[] for f in range(NF)]
    for j in range(3):
        cut = index[:, 128 * j : 128 * j + 128]
        tile, lane = lax.shift_right_arithmetic(cut, 7), cut & 127
        found = [jnp.zeros((8, 128), F32)] * NF
        for t in range(TILES):
            here = tile == t
            for f in range(NF):
                row = jnp.broadcast_to(first[t, f : f + 1, :], (8, 128))
                found[f] = jnp.where(here, jnp.take_along_axis(row, lane, axis=1), found[f])
        for f in range(NF):
            parts[f].append(found[f])
    return [jnp.concatenate(part, axis=1) for part in parts]


def step_kernel(
    first, state, velocity, bins, ymate, ynext, xmate, xnext, new_state_out, near_out, out,
    hi, lo, face_bins, face_lift, table, lifted, p, rows, acc, new_state, near_p, sems
):
    for k in range(16):
        pair = jnp.concatenate([first[2 * k], first[2 * k + 1]], axis=1)
        u, m, l = pieces_of(pair)
        block = jnp.concatenate([u[0:5], m[0:5], l[0:5], jnp.zeros((1, 256), F32)], axis=0)
        table[pl.ds(16 * k, 16), :] = block.astype(BF16)
    tab = table[...]
    time_step = COURANT / (1.0 + jnp.max(first[0, 6:7, :]))
    split_bins(bins, hi, lo)
    odd_y, odd_x = is_odd("box"), is_odd("depth")

    def lower(odd, mate, other):
        return jnp.where(odd, mate, other)

    def upper(odd, mate, other):
        return jnp.where(odd, other, mate)

    for x in range(X):
        face_bins[0, x : x + 1, :] = lower(odd_y, ymate[x, BN + 3 : BN + 4, :], ynext[x, BN + 3 : BN + 4, :]) - 1.0
        face_bins[1, x : x + 1, :] = upper(odd_y, ymate[x, BN : BN + 1, :], ynext[x, BN : BN + 1, :]) - 1.0
    face_bins[2] = lower(odd_x, xmate[BN + 3], xnext[BN + 3]) - 1.0
    face_bins[3] = upper(odd_x, xmate[BN], xnext[BN]) - 1.0

    def lift_some(i, carry):
        for k in range(2):
            x = 2 * i + k
            for y in range(Y):
                eight = lift_row(tab, hi[x, pl.ds(y, 1), :], lo[x, pl.ds(y, 1), :])
                for j in range(3):
                    lifted[x, j, pl.ds(8 * y, 8), :] = eight[:, 128 * j : 128 * j + 128]
        for f, value in enumerate(lift_five(first, face_bins[i])):
            face_lift[i, f] = value
        for k in range(2):
            x = 2 * i + k
            for f in range(NF):
                p[f, x + 1, pl.ds(8, 8), :] = state[f, x] - get_field(lifted, x, f)
        return carry

    lax.fori_loop(0, 4, lift_some, 0)
    for f in range(NF):
        p[f, 0, pl.ds(8, 8), :] = lower(odd_x, xmate[f], xnext[f]) - face_lift[2, f]
        p[f, X + 1, pl.ds(8, 8), :] = upper(odd_x, xmate[f], xnext[f]) - face_lift[3, f]
        for x in range(X):
            mate, other = ymate[x, f : f + 1, :], ynext[x, f : f + 1, :]
            p[f, x + 1, 7:8, :] = lower(odd_y, mate, other) - face_lift[0, f, x : x + 1, :]
            p[f, x + 1, 16:17, :] = upper(odd_y, mate, other) - face_lift[1, f, x : x + 1, :]

    acc[...] = jnp.zeros_like(acc)
    lane = lax.broadcasted_iota(jnp.int32, (Y, Z), 1)
    put_rows(rows, 15, jnp.zeros((Y, Z), F32))

    def advect(x, carry):
        v = [velocity[d, x] for d in range(3)]
        up = [jnp.maximum(c, 0.0) for c in v]
        down = [jnp.minimum(c, 0.0) for c in v]
        for f in range(NF):
            c = p[f, x + 1, pl.ds(8, 8), :]
            before = jnp.where(lane == 0, 0.0, pltpu.roll(c, 1, 1))
            after = jnp.where(lane == Z - 1, 0.0, pltpu.roll(c, Z - 1, 1))
            change = up[0] * (c - p[f, x, pl.ds(8, 8), :]) + down[0] * (p[f, x + 2, pl.ds(8, 8), :] - c)
            change += up[1] * (c - p[f, x + 1, pl.ds(7, 8), :]) + down[1] * (p[f, x + 1, pl.ds(9, 8), :] - c)
            change += up[2] * (c - before) + down[2] * (after - c)
            moved = c - time_step * change
            new_state[f, x] = get_field(lifted, x, f) + moved
            for i, piece in enumerate(pieces_of(moved)):
                put_rows(rows, NF * i + f, piece)
        state_copy(x).start()
        add_bins(acc, rows, hi, lo, x)
        return carry

    def state_copy(x):
        return pltpu.make_async_copy(new_state.at[:, x], new_state_out.at[:, x], sems.at[x])


    def gather_p(x, carry):
        total = WEIGHTS[0] * p[0, x]
        for f in range(1, NF):
            total += WEIGHTS[f] * p[f, x]
        near_p[x] = total
        return carry

    lax.fori_loop(0, X + 2, gather_p, 0)
    near_copy = pltpu.make_async_copy(near_p, near_out, sems.at[X])
    near_copy.start()
    lax.fori_loop(0, X, advect, 0)
    put_sums(out, acc, jnp.zeros((2, 256), F32))
    for x in range(X):
        state_copy(x).wait()
    near_copy.wait()


def weighted_rows(tiles):
    total = jnp.zeros((TILES, 128), F32)
    for f in range(NF):
        total += WEIGHTS[f] * tiles[:, f, :]
    return total


def row_table(total, pieces):
    return jnp.concatenate(pieces_of(total)[:pieces], axis=0).astype(BF16)


def lift_one(tab, b):
    high = jnp.floor(b * (1.0 / 128.0))
    low = b - 128.0 * high
    row = lax.broadcasted_iota(jnp.int32, (TILES, Z), 0).astype(F32)
    row16 = lax.broadcasted_iota(jnp.int32, (16, Z), 0).astype(F32).astype(BF16)
    one, zero = jnp.ones((16, Z), BF16), jnp.zeros((16, Z), BF16)
    wide = jnp.broadcast_to(low, (16, Z)).astype(BF16)
    t = jnp.concatenate([jnp.where(wide == row16 + jnp.asarray(16 * k, BF16), one, zero) for k in range(8)], axis=0)
    found = lax.dot_general(tab, t, (((1,), (0,)), ((), ())), preferred_element_type=F32)
    total = found[0:TILES]
    for i in range(1, tab.shape[0] // TILES):
        total += found[TILES * i : TILES * i + TILES]
    return jnp.sum(jnp.where(jnp.broadcast_to(high, (TILES, Z)) == row, total, 0.0), axis=0, keepdims=True)


def lift_eight(table, b):
    index = b.astype(jnp.int32)
    parts = []
    for j in range(3):
        cut = index[:, 128 * j : 128 * j + 128]
        tile, lane = lax.shift_right_arithmetic(cut, 7), cut & 127
        found = jnp.zeros((8, 128), F32)
        for t in range(TILES):
            row = jnp.broadcast_to(table[t : t + 1, :], (8, 128))
            found = jnp.where(tile == t, jnp.take_along_axis(row, lane, axis=1), found)
        parts.append(found)
    return jnp.concatenate(parts, axis=1)


def reach_rows(far):
    near = {0: range(7, 17), 1: range(8, 16)}
    return {d: [y for y in range(8 - far + d, 16 + far - d) if y not in near.get(d, ())] for d in range(far + 1)}


def ring_kernel(
    first, near_p, shifted, velocity, ymate, ynext, xmate, xnext, q_out, bins_out, p, q, high, v, faces, flat, sems, v_sems, out_sems
):
    def own():
        return [
            pltpu.make_async_copy(near_p, p.at[pl.ds(3, 10)], sems.at[0]),
            pltpu.make_async_copy(shifted, high.at[pl.ds(4, 8), pl.ds(8, 8)], sems.at[1]),
        ]

    def along_y(yhi, ylo):
        return [
            pltpu.make_async_copy(ylo, faces.at[0, pl.ds(0, 8)], sems.at[2]),
            pltpu.make_async_copy(yhi, faces.at[1, pl.ds(0, 8)], sems.at[3]),
        ]

    def along_x(xhi, xlo):
        blocks = [
            (xlo.at[pl.ds(SW, 3)], p.at[pl.ds(0, 3), pl.ds(8, 8)]),
            (xhi.at[pl.ds(SW + 1, 3)], p.at[pl.ds(13, 3), pl.ds(8, 8)]),
            (xlo.at[pl.ds(BN, 4)], high.at[pl.ds(0, 4), pl.ds(8, 8)]),
            (xhi.at[pl.ds(BN, 4)], high.at[pl.ds(12, 4), pl.ds(8, 8)]),
            (xlo.at[pl.ds(CSW, 12)], faces.at[2, pl.ds(0, 12), pl.ds(0, 8)]),
            (xhi.at[pl.ds(CSW, 12)], faces.at[3, pl.ds(0, 12), pl.ds(0, 8)]),
        ]
        return [pltpu.make_async_copy(src, dst, sems.at[4 + i]) for i, (src, dst) in enumerate(blocks)]

    def own_speed():
        return [pltpu.make_async_copy(velocity.at[d], v.at[d, pl.ds(3, 8), pl.ds(8, 8)], v_sems.at[d, 0]) for d in range(3)]

    def speed_x(xhi, xlo):
        copies = []
        for d in range(3):
            for i, (src, at) in enumerate(((xlo, 0), (xhi, 11))):
                src = src.at[pl.ds(VE + 3 * d, 3)]
                copies.append(pltpu.make_async_copy(src, v.at[d, pl.ds(at, 3), pl.ds(8, 8)], v_sems.at[d, 1 + i]))
        return copies

    for copy in own():
        copy.start()
    start_by(is_odd("box"), along_y, ymate, ynext)
    start_by(is_odd("depth"), along_x, xmate, xnext)
    for copy in own_speed():
        copy.start()
    start_by(is_odd("depth"), speed_x, xmate, xnext)
    early = own() + along_y(ymate, ynext) + along_x(xmate, xnext)
    late = own_speed() + speed_x(xmate, xnext)
    flat[...] = weighted_rows(first)
    tab = row_table(flat[...], 3)
    for copy in early:
        copy.wait()
    below, above, left, right = (faces.at[i] for i in range(4))
    p[pl.ds(4, 8), 4:7, :] = below[0:8, SW : SW + 3, :]
    p[pl.ds(4, 8), 17:20, :] = above[0:8, SW + 1 : SW + 4, :]
    high[pl.ds(4, 8), 4:8, :] = below[0:8, BN : BN + 4, :]
    high[pl.ds(4, 8), 16:20, :] = above[0:8, BN : BN + 4, :]
    for dst, corner in ((p, 0), (high, CBN - CSW)):
        for ref, at in ((left, 1), (right, 12)):
            dst[pl.ds(at, 3), 4:8, :] = ref[pl.ds(corner, 3), 0:4, :]
            dst[pl.ds(at, 3), 16:20, :] = ref[pl.ds(corner, 3), 4:8, :]
    bins_copy = pltpu.make_async_copy(high, bins_out, out_sems.at[0])
    bins_copy.start()
    rows = reach_rows(4)

    def lift_x(x, rows, block):
        if block:
            p[x, 8:16, :] = p[x, 8:16, :] - lift_eight(flat, high[x, 8:16, :] - 1.0)
        for y in rows:
            p[x, y : y + 1, :] = p[x, y : y + 1, :] - lift_one(tab, high[x, y : y + 1, :] - 1.0)

    def lift_sides(side, carry):
        for d in range(2, 5):
            lift_x((4 - d) + side * (7 + 2 * d), [y for y in rows[d] if not 8 <= y < 16], True)
        lift_x(3 + side * 9, rows[1], False)
        for i in range(4):
            lift_x(4 + 4 * side + i, rows[0], False)
        return carry

    lax.fori_loop(0, 2, lift_sides, 0)
    for copy in late:
        copy.wait()
    for d in range(3):
        row, corner = VE + 3 * d, CVE - CSW + 2 * d
        v[d, pl.ds(3, 8), 5:8, :] = below[0:8, row : row + 3, :]
        v[d, pl.ds(3, 8), 16:19, :] = above[0:8, row : row + 3, :]
        for ref, at in ((left, 1), (right, 11)):
            v[d, pl.ds(at, 2), 5:8, :] = ref[pl.ds(corner, 2), 0:3, :]
            v[d, pl.ds(at, 2), 16:19, :] = ref[pl.ds(corner, 2), 4:7, :]
    time_step = COURANT / (1.0 + jnp.max(first[0, 6:7, :]))
    lane = lax.broadcasted_iota(jnp.int32, (TALL, Z), 1)

    for x in range(14):
        c = p[x + 1]
        sides = (
            (p[x], p[x + 2]),
            (pltpu.roll(c, 1, 0), pltpu.roll(c, TALL - 1, 0)),
            (jnp.where(lane == 0, 0.0, pltpu.roll(c, 1, 1)), jnp.where(lane == Z - 1, 0.0, pltpu.roll(c, Z - 1, 1))),
        )
        change = jnp.zeros((TALL, Z), F32)
        for d, (before, after) in enumerate(sides):
            change += jnp.maximum(v[d, x], 0.0) * (c - before) + jnp.minimum(v[d, x], 0.0) * (after - c)
        q[x] = c - time_step * change
    q_copy = pltpu.make_async_copy(q, q_out, out_sems.at[1])
    q_copy.start()
    q_copy.wait()
    bins_copy.wait()


def relax_kernel(
    second_in, first_in, q_in, bins_in, potential_out, profile_out, src, high, pot, flat, second, first, potential, profile, sems, out_sems
):
    tables = [
        pltpu.make_async_copy(second_in, second, sems.at[4, 0]),
        pltpu.make_async_copy(first_in, first, sems.at[4, 1]),
    ]
    blocks = []
    for at, n in ((3, 4), (7, 4), (0, 3), (11, 3)):
        bins_at = pl.ds(at + 1, n)
        at = pl.ds(at, n)
        i = len(blocks)
        blocks.append([
            pltpu.make_async_copy(q_in.at[at], src.at[at], sems.at[i, 0]),
            pltpu.make_async_copy(bins_in.at[bins_at], high.at[bins_at], sems.at[i, 1]),
        ])
    for pair in [tables] + blocks:
        for copy in pair:
            copy.start()
    for copy in tables:
        copy.wait()
    flat[...] = weighted_rows(second)
    tab = row_table(flat[...], 2)
    for t in range(TILES):
        profile[:, 128 * t : 128 * t + 128] = (first[t] + second[t])[0:NF]
    profile_copy = pltpu.make_async_copy(profile, profile_out, out_sems.at[0])
    profile_copy.start()

    def lift_x(x, rows, block):
        if block:
            src[x, 8:16, :] = src[x, 8:16, :] - lift_eight(flat, high[x + 1, 8:16, :] - 1.0)
        for y in rows:
            src[x, y : y + 1, :] = src[x, y : y + 1, :] - lift_one(tab, high[x + 1, y : y + 1, :] - 1.0)
        scaled = src[x] * (OMEGA_RELAX / DIAGONAL)
        src[x] = scaled
        pot[0, x] = scaled

    def lift_sides(side, carry):
        for d in range(1, 4):
            rows = [y for y in range(5 + d, 19 - d) if d == 3 or not 8 <= y < 16]
            lift_x((3 - d) + side * (7 + 2 * d), rows, d < 3)
        return carry

    for h in range(2):
        for copy in blocks[h]:
            copy.wait()
        lax.fori_loop(3 + 4 * h, 7 + 4 * h, lambda x, c: (lift_x(x, (5, 6, 7, 16, 17, 18), True), c)[1], 0)
    for pair in blocks[2:]:
        for copy in pair:
            copy.wait()
    lax.fori_loop(0, 2, lift_sides, 0)
    lane = lax.broadcasted_iota(jnp.int32, (TALL, Z), 1)
    for s in range(1, 4):
        now, later = (s + 1) % 2, s % 2
        for x in range(s, 14 - s):
            c = pot[now, x]
            near = pot[now, x - 1] + pot[now, x + 1]
            near += pltpu.roll(c, 1, 0) + pltpu.roll(c, TALL - 1, 0)
            near += jnp.where(lane == 0, 0.0, pltpu.roll(c, 1, 1)) + jnp.where(lane == Z - 1, 0.0, pltpu.roll(c, Z - 1, 1))
            new = (1.0 - OMEGA_RELAX) * c + (src[x] + (OMEGA_RELAX / DIAGONAL) * near)
            if s < 3:
                pot[later, x] = jnp.where(high[x + 1] < 0.5, 0.0, new)
            else:
                potential[x - 3] = new[8:16]
    potential_copy = pltpu.make_async_copy(potential, potential_out, out_sems.at[1])
    potential_copy.start()
    potential_copy.wait()
    profile_copy.wait()


def f32_like(*shape):
    return jax.ShapeDtypeStruct(shape, F32)


def call(kernel, plan, *args):
    micros, out_shape, scratch, more = plan
    more = dict(more)
    limit = more.pop("megabytes") * 1024 * 1024
    return pl.pallas_call(
        kernel,
        out_shape=out_shape,
        cost_estimate=pl.CostEstimate(flops=micros * 1_000_000_000, bytes_accessed=0, transcendentals=0),
        scratch_shapes=[pltpu.VMEM(*part) if isinstance(part, tuple) else part for part in scratch],
        compiler_params=pltpu.CompilerParams(vmem_limit_bytes=limit),
        **more,
    )(*args)


def exchange(to_mate, to_next, axis):
    count = lax.axis_size(axis)
    mates = [(i, i ^ 1) for i in range(count)]
    others = [pair for i in range(1, count - 1, 2) for pair in ((i, i + 1), (i + 1, i))]
    return lax.ppermute(to_mate, axis, mates), lax.ppermute(to_next, axis, others)


def added(tiles):
    total, top = tiles[0], tiles[0]
    for i in range(1, MEMBERS):
        total, top = total + tiles[i], jnp.maximum(top, tiles[i])
    return jnp.where(lax.broadcasted_iota(jnp.int32, total.shape, 1) == 6, top, total)


def merge_kernel(tiles, share, copies):
    total = added(tiles)
    share[...] = total
    for i in range(MEMBERS):
        copies[i] = total


def divide_kernel(tiles, counts, share, copies):
    total = added(tiles)
    cells = total if counts is None else counts
    row = lax.broadcasted_iota(jnp.int32, total.shape, 1)
    mean = jnp.where(row < NF, total / jnp.maximum(cells[:, 5:6, :], 1.0), total)
    share[...] = total
    for i in range(MEMBERS):
        copies[i] = mean


def divide_own_kernel(tiles, share, copies):
    divide_kernel(tiles, None, share, copies)


def groups_of(varied):
    sizes = (4, 8, 4, 2)
    fixed = [d for d in range(4) if d not in varied]
    places = np.arange(256).reshape(sizes).transpose(fixed + list(varied))
    return places.reshape(-1, math.prod(sizes[d] for d in varied)).tolist()


SHARE_GROUPS = groups_of((0, 2))
OTHER_GROUPS = groups_of((1, 3))
def swap(parts, groups):
    return lax.all_to_all(parts, ("box", "depth"), 0, 0, axis_index_groups=groups, tiled=True)


def in_members(tiles):
    return tiles.reshape(MEMBERS, TILES // MEMBERS, 8, 128)


VISIBLE = pl.BlockSpec(memory_space=pltpu.VMEM)
REMOTE = pl.BlockSpec(memory_space=pl.ANY)
SUMS = (
    7,
    tuple(pltpu.HBM(shape, F32) for shape in ((X, TALL, Z), (X, TALL, Z), (X, Y, Z), (X, Y, Z))) + (f32_like(TILES, 8, 128),),
    [
        ((X, Y, Z), F32), ((X, Y, Z), F32), ((3, Y * 16, 128), F32), ((256, 256), F32),
        ((NF, X, Y, Z), F32), ((3, X, Y, Z), F32), ((X, Y, Z), jnp.int32),
        ((X, TALL, Z), F32), ((X, TALL, Z), F32), ((X, Y, Z), F32), ((X, Y, Z), F32),
        pltpu.SemaphoreType.DMA((5, 2)), pltpu.SemaphoreType.DMA((2, 4)),
    ],
    dict(in_specs=[REMOTE] * 3, out_specs=(REMOTE,) * 4 + (VISIBLE,), megabytes=58),
)
PACK_X = (
    2,
    (f32_like(PLANES, Y, Z), f32_like(PLANES, Y, Z)),
    [((2, PLANES - CSW, Y, Z), F32), pltpu.SemaphoreType.DMA((2, 7))],
    dict(in_specs=[REMOTE] * 4 + [VISIBLE] * 2, out_specs=(REMOTE, REMOTE), megabytes=20),
)
STEP = (
    14,
    (f32_like(NF, X, Y, Z), pltpu.HBM((X + 2, TALL, Z), F32), f32_like(TILES, 8, 128)),
    [
        ((X, Y, Z), F32), ((X, Y, Z), F32), ((4, Y, Z), F32), ((4, NF, Y, Z), F32), ((256, 256), BF16),
        ((X, 3, 64, 128), F32), ((NF, X + 2, TALL, Z), F32), ((3, Y * 16, 128), F32), ((256, 256), F32),
        ((NF, X, Y, Z), F32), ((X + 2, TALL, Z), F32), pltpu.SemaphoreType.DMA((X + 1,)),
    ],
    dict(out_specs=(REMOTE, REMOTE, VISIBLE), megabytes=24),
)
RING = (
    8,
    (f32_like(14, TALL, Z), f32_like(16, TALL, Z)),
    [
        ((16, TALL, Z), F32), ((14, TALL, Z), F32), ((16, TALL, Z), F32), ((3, 14, TALL, Z), F32), ((4, 12, TALL, Z), F32), ((TILES, 128), F32),
        pltpu.SemaphoreType.DMA((10,)), pltpu.SemaphoreType.DMA((3, 3)), pltpu.SemaphoreType.DMA((2,)),
    ],
    dict(in_specs=[VISIBLE] + [REMOTE] * 7, out_specs=(REMOTE, REMOTE), megabytes=58),
)
RELAX = (
    9,
    (pltpu.HBM((X, Y, Z), F32), pltpu.HBM((NF, NBINS), F32)),
    [
        ((14, TALL, Z), F32), ((16, TALL, Z), F32), ((2, 14, TALL, Z), F32), ((TILES, 128), F32),
        ((TILES, 8, 128), F32), ((TILES, 8, 128), F32), ((X, Y, Z), F32), ((NF, NBINS), F32),
        pltpu.SemaphoreType.DMA((5, 2)), pltpu.SemaphoreType.DMA((2,)),
    ],
    dict(in_specs=[REMOTE] * 4, out_specs=(REMOTE, REMOTE), megabytes=58),
)


MERGE = (0, (f32_like(2, 8, 128), f32_like(MEMBERS, 2, 8, 128)), [], dict(megabytes=20))


def per_device(state, velocity, bins):
    to_mate, to_next, weighted, shifted, tiles = call(sums_kernel, SUMS, state, velocity, bins)
    ymate, ynext = exchange(to_mate, to_next, "box")
    to_mate, to_next = call(pack_x_kernel, PACK_X, state, velocity, weighted, shifted, ymate, ynext)
    xmate, xnext = exchange(to_mate, to_next, "depth")
    share, copies = call(merge_kernel, MERGE, swap(in_members(tiles), SHARE_GROUPS))
    share, copies = call(divide_own_kernel, MERGE, swap(copies, OTHER_GROUPS))
    first = swap(copies, SHARE_GROUPS).reshape(TILES, 8, 128)
    new_state, near_p, tiles = call(step_kernel, STEP, first, state, velocity, bins, ymate, ynext, xmate, xnext)
    q, wide_bins = call(ring_kernel, RING, first, near_p, shifted, velocity, ymate, ynext, xmate, xnext)
    part, copies = call(merge_kernel, MERGE, swap(in_members(tiles), SHARE_GROUPS))
    copies, q, wide_bins = lax.optimization_barrier((copies, q, wide_bins))
    part, copies = call(divide_kernel, MERGE, swap(copies, OTHER_GROUPS), share)
    second = swap(copies, SHARE_GROUPS).reshape(TILES, 8, 128)
    potential, profile = call(relax_kernel, RELAX, second, first, q, wide_bins)
    return (new_state, potential, profile)


def solution(mesh):
    return jax.shard_map(
        per_device,
        mesh=mesh,
        in_specs=(
            P(None, "depth", "box", None),
            P(None, "depth", "box", None),
            P("depth", "box", None),
        ),
        out_specs=(P(None, "depth", "box", None), P("depth", "box", None), P()),
        check_vma=False,
    )
```

```python
import functools
import math

import jax
import jax.numpy as jnp
import numpy as np
from jax import lax
from jax.experimental import pallas as pl
from jax.experimental.pallas import tpu as pltpu
from jax.sharding import PartitionSpec as P

NBINS = 4096
COURANT = 0.8
OMEGA_RELAX = 0.8
DIAGONAL = 6.1
WEIGHTS = (1.0, 0.5, -0.5, 0.25, 0.75)
NF = 5
X, Y, Z = 8, 8, 384
TILES = NBINS // 128
SW, BN, VE, CSW, CBN, CVE, PLANES = 5, 9, 13, 22, 25, 28, 34
TALL = 24
MEMBERS = 16
F32, BF16 = jnp.float32, jnp.bfloat16


def pieces_of(values):
    upper = values.astype(BF16).astype(F32)
    rest = values - upper
    middle = rest.astype(BF16).astype(F32)
    return upper, middle, rest - middle


def lo_table(lo_row):
    wide = jnp.broadcast_to(lo_row, (16, Z)).astype(BF16)
    row = lax.broadcasted_iota(jnp.int32, (16, Z), 0).astype(F32).astype(BF16)
    one, zero = jnp.ones((16, Z), BF16), jnp.zeros((16, Z), BF16)
    return jnp.concatenate([jnp.where(wide == row + jnp.asarray(16 * k, BF16), one, zero) for k in range(16)], axis=0)


def hi_rows(hi_row, rows16):
    wide = jnp.broadcast_to(hi_row, (16, Z)).astype(BF16)
    zero = jnp.zeros((16, Z), BF16)
    return jnp.concatenate([jnp.where(wide == jnp.asarray(k, BF16), rows16, zero) for k in range(16)], axis=0)


def put_rows(rows, p, values):
    for j in range(3):
        rows[j, pl.ds(p, Y, stride=16), :] = values[:, j * 128 : (j + 1) * 128]


def get_rows(rows, y):
    return jnp.concatenate([rows[j, pl.ds(16 * y, 16), :].astype(BF16) for j in range(3)], axis=1)


def get_field(lifted, x, f):
    return jnp.concatenate([lifted[x, j, pl.ds(f, Y, stride=8), :] for j in range(3)], axis=1)


def add_bins(acc, rows, hi, lo, x):
    left, right = [], []
    for y in range(Y):
        left.append(hi_rows(hi[x, pl.ds(y, 1), :], get_rows(rows, y)))
        right.append(lo_table(lo[x, pl.ds(y, 1), :]))
    acc[...] += lax.dot_general(
        jnp.concatenate(left, 1), jnp.concatenate(right, 1), (((1,), (1,)), ((), ())), preferred_element_type=F32
    )


def put_sums(out, acc, extra):
    for k in range(16):
        s = acc[pl.ds(16 * k, 16), :]
        tile = jnp.concatenate([s[0:5] + s[5:10] + s[10:15], s[15:16], extra], axis=0)
        out[2 * k] = tile[:, :128]
        out[2 * k + 1] = tile[:, 128:]


def split_bins(bins, hi, lo):
    b = bins[...]
    hi[...] = lax.shift_right_logical(b, 8).astype(F32)
    lo[...] = (b & 255).astype(F32)


def is_odd(axis):
    return lax.rem(lax.axis_index(axis), 2) == 1


def start_by(odd, make, even_place, odd_place):
    @pl.when(jnp.logical_not(odd))
    def _():
        for copy in make(even_place, odd_place):
            copy.start()

    @pl.when(odd)
    def _():
        for copy in make(odd_place, even_place):
            copy.start()


def sums_kernel(
    state_in, velocity_in, bins_in, mate_out, next_out, weighted_out, shifted_out, tiles_out,
    hi, lo, rows, acc, state, velocity, bins, to_above, to_below, weighted, shifted, out, sems, out_sems
):
    bins_copy = pltpu.make_async_copy(bins_in, bins, sems.at[4, 0])
    bins_copy.start()

    def arrive(h):
        at = pl.ds(2 * h, 2)
        return [
            pltpu.make_async_copy(state_in.at[:, at], state.at[:, at], sems.at[h, 0]),
            pltpu.make_async_copy(velocity_in.at[:, at], velocity.at[:, at], sems.at[h, 1]),
        ]

    def leave(h, above_out, below_out):
        at = pl.ds(2 * h, 2)
        pairs = ((to_above, above_out), (to_below, below_out), (weighted, weighted_out), (shifted, shifted_out))
        return [pltpu.make_async_copy(src.at[at], dst.at[at], out_sems.at[h, i]) for i, (src, dst) in enumerate(pairs)]

    for h in range(4):
        for copy in arrive(h):
            copy.start()
    acc[...] = jnp.zeros_like(acc)
    put_rows(rows, 15, jnp.ones((Y, Z), F32))
    bins_copy.wait()
    split_bins(bins, hi, lo)
    shifted[...] = bins[...].astype(F32) + 1.0

    def step(x, top):
        s = [state[f, x] for f in range(NF)]
        w = WEIGHTS[0] * s[0]
        for f in range(NF):
            for i, piece in enumerate(pieces_of(s[f])):
                put_rows(rows, NF * i + f, piece)
            if f > 0:
                w += WEIGHTS[f] * s[f]
        add_bins(acc, rows, hi, lo, x)
        weighted[x] = w
        b = shifted[x]
        v = [velocity[d, x] for d in range(3)]
        for face, near, four, three in ((to_above, Y - 1, Y - 4, Y - 3), (to_below, 0, 0, 0)):
            parts = [c[near : near + 1] for c in s] + [w[four : four + 4], b[four : four + 4]]
            parts += [c[three : three + 3] for c in v] + [jnp.zeros((2, Z), F32)]
            face[x] = jnp.concatenate(parts, axis=0)
        return jnp.maximum(top, jnp.abs(v[0]) + jnp.abs(v[1]) + jnp.abs(v[2]))

    top = jnp.zeros((Y, Z), F32)
    def two(h, top):
        for copy in arrive(h):
            copy.wait()
        top = step(2 * h + 1, step(2 * h, top))
        start_by(is_odd("box"), functools.partial(leave, h), mate_out, next_out)
        return top

    top = lax.fori_loop(0, 4, two, top)
    put_sums(out, acc, jnp.full((2, 256), jnp.max(top), F32))
    tiles_copy = pltpu.make_async_copy(out, tiles_out, sems.at[4, 1])
    tiles_copy.start()
    tiles_copy.wait()
    for h in range(4):
        for copy in leave(h, mate_out, next_out):
            copy.wait()


def pack_x_kernel(state, velocity, weighted, shifted, ymate, ynext, mate_out, next_out, corners, sems):
    def fill(to_above, to_below):
        copies = []
        for side, (out, near, four, three) in enumerate(((to_above, X - 1, X - 4, X - 3), (to_below, 0, 0, 0))):
            parts = [(state.at[:, near], 0, NF), (weighted.at[pl.ds(four, 4)], SW, 4), (shifted.at[pl.ds(four, 4)], BN, 4)]
            parts += [(velocity.at[d, pl.ds(three, 3)], VE + 3 * d, 3) for d in range(3)]
            for i, (src, at, n) in enumerate(parts):
                copies.append(pltpu.make_async_copy(src, out.at[pl.ds(at, n)], sems.at[side, i]))
        return copies

    def fill_corners(to_above, to_below):
        return [
            pltpu.make_async_copy(corners.at[side], out.at[pl.ds(CSW, PLANES - CSW)], sems.at[side, 6])
            for side, out in enumerate((to_above, to_below))
        ]

    start_by(is_odd("depth"), fill, mate_out, next_out)
    odd = is_odd("box")
    gap = jnp.zeros((1, Z), F32)
    for side, (three, two) in enumerate(((X - 3, X - 2), (0, 0))):
        for x in range(three, three + 3):
            ylo, yhi = jnp.where(odd, ymate[x], ynext[x]), jnp.where(odd, ynext[x], ymate[x])
            for at, row in ((CSW, SW), (CBN, BN)):
                corners[side, at - CSW + x - three] = jnp.concatenate([ylo[row : row + 4], yhi[row : row + 4]], axis=0)
            if 0 <= x - two < 2:
                for d in range(3):
                    row = VE + 3 * d
                    corners[side, CVE - CSW + 2 * d + x - two] = jnp.concatenate(
                        [ylo[row : row + 3], gap, yhi[row : row + 3], gap], axis=0
                    )
    start_by(is_odd("depth"), fill_corners, mate_out, next_out)
    for copy in fill(mate_out, next_out) + fill_corners(mate_out, next_out):
        copy.wait()


def lift_row(table, hi_row, lo_row):
    found = lax.dot_general(table, lo_table(lo_row), (((1,), (0,)), ((), ())), preferred_element_type=F32)
    wide = jnp.broadcast_to(hi_row, (16, Z))
    acc = jnp.zeros((16, Z), F32)
    for k in range(16):
        acc = jnp.where(wide == float(k), found[16 * k : 16 * k + 16], acc)
    total = acc[0:5] + acc[5:10] + acc[10:15]
    return jnp.concatenate([total, jnp.zeros((3, Z), F32)], axis=0)


def lift_five(first, b):
    index = b.astype(jnp.int32)
    parts = [[] for f in range(NF)]
    for j in range(3):
        cut = index[:, 128 * j : 128 * j + 128]
        tile, lane = lax.shift_right_arithmetic(cut, 7), cut & 127
        found = [jnp.zeros((8, 128), F32)] * NF
        for t in range(TILES):
            here = tile == t
            for f in range(NF):
                row = jnp.broadcast_to(first[t, f : f + 1, :], (8, 128))
                found[f] = jnp.where(here, jnp.take_along_axis(row, lane, axis=1), found[f])
        for f in range(NF):
            parts[f].append(found[f])
    return [jnp.concatenate(part, axis=1) for part in parts]


def step_kernel(
    first, state, velocity, bins, ymate, ynext, xmate, xnext, new_state_out, near_out, out,
    hi, lo, face_bins, face_lift, table, lifted, p, rows, acc, new_state, near_p, sems
):
    for k in range(16):
        pair = jnp.concatenate([first[2 * k], first[2 * k + 1]], axis=1)
        u, m, l = pieces_of(pair)
        block = jnp.concatenate([u[0:5], m[0:5], l[0:5], jnp.zeros((1, 256), F32)], axis=0)
        table[pl.ds(16 * k, 16), :] = block.astype(BF16)
    tab = table[...]
    time_step = COURANT / (1.0 + jnp.max(first[0, 6:7, :]))
    split_bins(bins, hi, lo)
    odd_y, odd_x = is_odd("box"), is_odd("depth")

    def lower(odd, mate, other):
        return jnp.where(odd, mate, other)

    def upper(odd, mate, other):
        return jnp.where(odd, other, mate)

    for x in range(X):
        face_bins[0, x : x + 1, :] = lower(odd_y, ymate[x, BN + 3 : BN + 4, :], ynext[x, BN + 3 : BN + 4, :]) - 1.0
        face_bins[1, x : x + 1, :] = upper(odd_y, ymate[x, BN : BN + 1, :], ynext[x, BN : BN + 1, :]) - 1.0
    face_bins[2] = lower(odd_x, xmate[BN + 3], xnext[BN + 3]) - 1.0
    face_bins[3] = upper(odd_x, xmate[BN], xnext[BN]) - 1.0

    def lift_some(i, carry):
        for k in range(2):
            x = 2 * i + k
            for y in range(Y):
                eight = lift_row(tab, hi[x, pl.ds(y, 1), :], lo[x, pl.ds(y, 1), :])
                for j in range(3):
                    lifted[x, j, pl.ds(8 * y, 8), :] = eight[:, 128 * j : 128 * j + 128]
        for f, value in enumerate(lift_five(first, face_bins[i])):
            face_lift[i, f] = value
        for k in range(2):
            x = 2 * i + k
            for f in range(NF):
                p[f, x + 1, pl.ds(8, 8), :] = state[f, x] - get_field(lifted, x, f)
        return carry

    for i in range(4):
        lift_some(i, 0)
    for f in range(NF):
        p[f, 0, pl.ds(8, 8), :] = lower(odd_x, xmate[f], xnext[f]) - face_lift[2, f]
        p[f, X + 1, pl.ds(8, 8), :] = upper(odd_x, xmate[f], xnext[f]) - face_lift[3, f]
        for x in range(X):
            mate, other = ymate[x, f : f + 1, :], ynext[x, f : f + 1, :]
            p[f, x + 1, 7:8, :] = lower(odd_y, mate, other) - face_lift[0, f, x : x + 1, :]
            p[f, x + 1, 16:17, :] = upper(odd_y, mate, other) - face_lift[1, f, x : x + 1, :]

    acc[...] = jnp.zeros_like(acc)
    lane = lax.broadcasted_iota(jnp.int32, (Y, Z), 1)
    put_rows(rows, 15, jnp.zeros((Y, Z), F32))

    def advect(x, carry):
        v = [velocity[d, x] for d in range(3)]
        up = [jnp.maximum(c, 0.0) for c in v]
        down = [jnp.minimum(c, 0.0) for c in v]
        for f in range(NF):
            c = p[f, x + 1, pl.ds(8, 8), :]
            before = jnp.where(lane == 0, 0.0, pltpu.roll(c, 1, 1))
            after = jnp.where(lane == Z - 1, 0.0, pltpu.roll(c, Z - 1, 1))
            change = up[0] * (c - p[f, x, pl.ds(8, 8), :]) + down[0] * (p[f, x + 2, pl.ds(8, 8), :] - c)
            change += up[1] * (c - p[f, x + 1, pl.ds(7, 8), :]) + down[1] * (p[f, x + 1, pl.ds(9, 8), :] - c)
            change += up[2] * (c - before) + down[2] * (after - c)
            moved = c - time_step * change
            new_state[f, x] = get_field(lifted, x, f) + moved
            for i, piece in enumerate(pieces_of(moved)):
                put_rows(rows, NF * i + f, piece)
        state_copy(x).start()
        add_bins(acc, rows, hi, lo, x)
        return carry

    def state_copy(x):
        return pltpu.make_async_copy(new_state.at[:, x], new_state_out.at[:, x], sems.at[x])


    for x in range(X + 2):
        total = WEIGHTS[0] * p[0, x]
        for f in range(1, NF):
            total += WEIGHTS[f] * p[f, x]
        near_p[x] = total
    near_copy = pltpu.make_async_copy(near_p, near_out, sems.at[X])
    near_copy.start()
    lax.fori_loop(0, X // 2, lambda i, c: advect(2 * i + 1, advect(2 * i, c)), 0)
    put_sums(out, acc, jnp.zeros((2, 256), F32))
    for x in range(X):
        state_copy(x).wait()
    near_copy.wait()


def weighted_rows(tiles):
    total = jnp.zeros((TILES, 128), F32)
    for f in range(NF):
        total += WEIGHTS[f] * tiles[:, f, :]
    return total


def row_table(total, pieces):
    return jnp.concatenate(pieces_of(total)[:pieces], axis=0).astype(BF16)


def lift_one(tab, b):
    high = jnp.floor(b * (1.0 / 128.0))
    low = b - 128.0 * high
    row = lax.broadcasted_iota(jnp.int32, (TILES, Z), 0).astype(F32)
    row16 = lax.broadcasted_iota(jnp.int32, (16, Z), 0).astype(F32).astype(BF16)
    one, zero = jnp.ones((16, Z), BF16), jnp.zeros((16, Z), BF16)
    wide = jnp.broadcast_to(low, (16, Z)).astype(BF16)
    t = jnp.concatenate([jnp.where(wide == row16 + jnp.asarray(16 * k, BF16), one, zero) for k in range(8)], axis=0)
    found = lax.dot_general(tab, t, (((1,), (0,)), ((), ())), preferred_element_type=F32)
    total = found[0:TILES]
    for i in range(1, tab.shape[0] // TILES):
        total += found[TILES * i : TILES * i + TILES]
    return jnp.sum(jnp.where(jnp.broadcast_to(high, (TILES, Z)) == row, total, 0.0), axis=0, keepdims=True)


def lift_eight(table, b):
    index = b.astype(jnp.int32)
    parts = []
    for j in range(3):
        cut = index[:, 128 * j : 128 * j + 128]
        tile, lane = lax.shift_right_arithmetic(cut, 7), cut & 127
        found = jnp.zeros((8, 128), F32)
        for t in range(TILES):
            row = jnp.broadcast_to(table[t : t + 1, :], (8, 128))
            found = jnp.where(tile == t, jnp.take_along_axis(row, lane, axis=1), found)
        parts.append(found)
    return jnp.concatenate(parts, axis=1)


def reach_rows(far):
    near = {0: range(7, 17), 1: range(8, 16)}
    return {d: [y for y in range(8 - far + d, 16 + far - d) if y not in near.get(d, ())] for d in range(far + 1)}


def ring_kernel(
    first, near_p, shifted, velocity, ymate, ynext, xmate, xnext, q_out, bins_out, p, q, high, v, faces, flat, sems, v_sems, out_sems
):
    def own():
        return [
            pltpu.make_async_copy(near_p, p.at[pl.ds(3, 10)], sems.at[0]),
            pltpu.make_async_copy(shifted, high.at[pl.ds(4, 8), pl.ds(8, 8)], sems.at[1]),
        ]

    def along_y(yhi, ylo):
        return [
            pltpu.make_async_copy(ylo, faces.at[0, pl.ds(0, 8)], sems.at[2]),
            pltpu.make_async_copy(yhi, faces.at[1, pl.ds(0, 8)], sems.at[3]),
        ]

    def along_x(xhi, xlo):
        blocks = [
            (xlo.at[pl.ds(SW, 3)], p.at[pl.ds(0, 3), pl.ds(8, 8)]),
            (xhi.at[pl.ds(SW + 1, 3)], p.at[pl.ds(13, 3), pl.ds(8, 8)]),
            (xlo.at[pl.ds(BN, 4)], high.at[pl.ds(0, 4), pl.ds(8, 8)]),
            (xhi.at[pl.ds(BN, 4)], high.at[pl.ds(12, 4), pl.ds(8, 8)]),
            (xlo.at[pl.ds(CSW, 12)], faces.at[2, pl.ds(0, 12), pl.ds(0, 8)]),
            (xhi.at[pl.ds(CSW, 12)], faces.at[3, pl.ds(0, 12), pl.ds(0, 8)]),
        ]
        return [pltpu.make_async_copy(src, dst, sems.at[4 + i]) for i, (src, dst) in enumerate(blocks)]

    def own_speed():
        return [pltpu.make_async_copy(velocity.at[d], v.at[d, pl.ds(3, 8), pl.ds(8, 8)], v_sems.at[d, 0]) for d in range(3)]

    def speed_x(xhi, xlo):
        copies = []
        for d in range(3):
            for i, (src, at) in enumerate(((xlo, 0), (xhi, 11))):
                src = src.at[pl.ds(VE + 3 * d, 3)]
                copies.append(pltpu.make_async_copy(src, v.at[d, pl.ds(at, 3), pl.ds(8, 8)], v_sems.at[d, 1 + i]))
        return copies

    for copy in own():
        copy.start()
    start_by(is_odd("box"), along_y, ymate, ynext)
    start_by(is_odd("depth"), along_x, xmate, xnext)
    for copy in own_speed():
        copy.start()
    start_by(is_odd("depth"), speed_x, xmate, xnext)
    early = own() + along_y(ymate, ynext) + along_x(xmate, xnext)
    late = own_speed() + speed_x(xmate, xnext)
    flat[...] = weighted_rows(first)
    tab = row_table(flat[...], 3)
    for copy in early:
        copy.wait()
    below, above, left, right = (faces.at[i] for i in range(4))
    p[pl.ds(4, 8), 4:7, :] = below[0:8, SW : SW + 3, :]
    p[pl.ds(4, 8), 17:20, :] = above[0:8, SW + 1 : SW + 4, :]
    high[pl.ds(4, 8), 4:8, :] = below[0:8, BN : BN + 4, :]
    high[pl.ds(4, 8), 16:20, :] = above[0:8, BN : BN + 4, :]
    for dst, corner in ((p, 0), (high, CBN - CSW)):
        for ref, at in ((left, 1), (right, 12)):
            dst[pl.ds(at, 3), 4:8, :] = ref[pl.ds(corner, 3), 0:4, :]
            dst[pl.ds(at, 3), 16:20, :] = ref[pl.ds(corner, 3), 4:8, :]
    bins_copy = pltpu.make_async_copy(high, bins_out, out_sems.at[0])
    bins_copy.start()
    rows = reach_rows(4)

    def lift_x(x, rows, block):
        if block:
            p[x, 8:16, :] = p[x, 8:16, :] - lift_eight(flat, high[x, 8:16, :] - 1.0)
        for y in rows:
            p[x, y : y + 1, :] = p[x, y : y + 1, :] - lift_one(tab, high[x, y : y + 1, :] - 1.0)

    def lift_sides(side, carry):
        for d in range(2, 5):
            lift_x((4 - d) + side * (7 + 2 * d), [y for y in rows[d] if not 8 <= y < 16], True)
        lift_x(3 + side * 9, rows[1], False)
        for i in range(4):
            lift_x(4 + 4 * side + i, rows[0], False)
        return carry

    for side in range(2):
        lift_sides(side, 0)
    for copy in late:
        copy.wait()
    for d in range(3):
        row, corner = VE + 3 * d, CVE - CSW + 2 * d
        v[d, pl.ds(3, 8), 5:8, :] = below[0:8, row : row + 3, :]
        v[d, pl.ds(3, 8), 16:19, :] = above[0:8, row : row + 3, :]
        for ref, at in ((left, 1), (right, 11)):
            v[d, pl.ds(at, 2), 5:8, :] = ref[pl.ds(corner, 2), 0:3, :]
            v[d, pl.ds(at, 2), 16:19, :] = ref[pl.ds(corner, 2), 4:7, :]
    time_step = COURANT / (1.0 + jnp.max(first[0, 6:7, :]))
    lane = lax.broadcasted_iota(jnp.int32, (TALL, Z), 1)

    for x in range(14):
        c = p[x + 1]
        sides = (
            (p[x], p[x + 2]),
            (pltpu.roll(c, 1, 0), pltpu.roll(c, TALL - 1, 0)),
            (jnp.where(lane == 0, 0.0, pltpu.roll(c, 1, 1)), jnp.where(lane == Z - 1, 0.0, pltpu.roll(c, Z - 1, 1))),
        )
        change = jnp.zeros((TALL, Z), F32)
        for d, (before, after) in enumerate(sides):
            change += jnp.maximum(v[d, x], 0.0) * (c - before) + jnp.minimum(v[d, x], 0.0) * (after - c)
        q[x] = c - time_step * change
    q_copy = pltpu.make_async_copy(q, q_out, out_sems.at[1])
    q_copy.start()
    q_copy.wait()
    bins_copy.wait()


def relax_kernel(
    second_in, first_in, q_in, bins_in, potential_out, profile_out, src, high, pot, flat, second, first, potential, profile, sems, out_sems
):
    tables = [
        pltpu.make_async_copy(second_in, second, sems.at[4, 0]),
        pltpu.make_async_copy(first_in, first, sems.at[4, 1]),
    ]
    blocks = []
    for at, n in ((3, 4), (7, 4), (0, 3), (11, 3)):
        bins_at = pl.ds(at + 1, n)
        at = pl.ds(at, n)
        i = len(blocks)
        blocks.append([
            pltpu.make_async_copy(q_in.at[at], src.at[at], sems.at[i, 0]),
            pltpu.make_async_copy(bins_in.at[bins_at], high.at[bins_at], sems.at[i, 1]),
        ])
    for pair in [tables] + blocks:
        for copy in pair:
            copy.start()
    for copy in tables:
        copy.wait()
    flat[...] = weighted_rows(second)
    tab = row_table(flat[...], 2)
    for t in range(TILES):
        profile[:, 128 * t : 128 * t + 128] = (first[t] + second[t])[0:NF]
    profile_copy = pltpu.make_async_copy(profile, profile_out, out_sems.at[0])
    profile_copy.start()

    def lift_x(x, rows, block):
        if block:
            src[x, 8:16, :] = src[x, 8:16, :] - lift_eight(flat, high[x + 1, 8:16, :] - 1.0)
        for y in rows:
            src[x, y : y + 1, :] = src[x, y : y + 1, :] - lift_one(tab, high[x + 1, y : y + 1, :] - 1.0)
        scaled = src[x] * (OMEGA_RELAX / DIAGONAL)
        src[x] = scaled
        pot[0, x] = scaled

    def lift_sides(side, carry):
        for d in range(1, 4):
            rows = [y for y in range(5 + d, 19 - d) if d == 3 or not 8 <= y < 16]
            lift_x((3 - d) + side * (7 + 2 * d), rows, d < 3)
        return carry

    for h in range(2):
        for copy in blocks[h]:
            copy.wait()
        for x in range(3 + 4 * h, 7 + 4 * h):
            lift_x(x, (5, 6, 7, 16, 17, 18), True)
    for pair in blocks[2:]:
        for copy in pair:
            copy.wait()
    for side in range(2):
        lift_sides(side, 0)
    lane = lax.broadcasted_iota(jnp.int32, (TALL, Z), 1)
    for s in range(1, 4):
        now, later = (s + 1) % 2, s % 2
        for x in range(s, 14 - s):
            c = pot[now, x]
            near = pot[now, x - 1] + pot[now, x + 1]
            near += pltpu.roll(c, 1, 0) + pltpu.roll(c, TALL - 1, 0)
            near += jnp.where(lane == 0, 0.0, pltpu.roll(c, 1, 1)) + jnp.where(lane == Z - 1, 0.0, pltpu.roll(c, Z - 1, 1))
            new = (1.0 - OMEGA_RELAX) * c + (src[x] + (OMEGA_RELAX / DIAGONAL) * near)
            if s < 3:
                pot[later, x] = jnp.where(high[x + 1] < 0.5, 0.0, new)
            else:
                potential[x - 3] = new[8:16]
    potential_copy = pltpu.make_async_copy(potential, potential_out, out_sems.at[1])
    potential_copy.start()
    potential_copy.wait()
    profile_copy.wait()


def f32_like(*shape):
    return jax.ShapeDtypeStruct(shape, F32)


def call(kernel, plan, *args):
    micros, out_shape, scratch, more = plan
    more = dict(more)
    limit = more.pop("megabytes") * 1024 * 1024
    return pl.pallas_call(
        kernel,
        out_shape=out_shape,
        cost_estimate=pl.CostEstimate(flops=micros * 1_000_000_000, bytes_accessed=0, transcendentals=0),
        scratch_shapes=[pltpu.VMEM(*part) if isinstance(part, tuple) else part for part in scratch],
        compiler_params=pltpu.CompilerParams(vmem_limit_bytes=limit),
        **more,
    )(*args)


def exchange(to_mate, to_next, axis):
    count = lax.axis_size(axis)
    mates = [(i, i ^ 1) for i in range(count)]
    others = [pair for i in range(1, count - 1, 2) for pair in ((i, i + 1), (i + 1, i))]
    return lax.ppermute(to_mate, axis, mates), lax.ppermute(to_next, axis, others)


def added(tiles):
    total, top = tiles[0], tiles[0]
    for i in range(1, MEMBERS):
        total, top = total + tiles[i], jnp.maximum(top, tiles[i])
    return jnp.where(lax.broadcasted_iota(jnp.int32, total.shape, 1) == 6, top, total)


def merge_kernel(tiles, share, copies):
    total = added(tiles)
    share[...] = total
    for i in range(MEMBERS):
        copies[i] = total


def divide_kernel(tiles, counts, share, copies):
    total = added(tiles)
    cells = total if counts is None else counts
    row = lax.broadcasted_iota(jnp.int32, total.shape, 1)
    mean = jnp.where(row < NF, total / jnp.maximum(cells[:, 5:6, :], 1.0), total)
    share[...] = total
    for i in range(MEMBERS):
        copies[i] = mean


def divide_own_kernel(tiles, share, copies):
    divide_kernel(tiles, None, share, copies)


def groups_of(varied):
    sizes = (4, 8, 4, 2)
    fixed = [d for d in range(4) if d not in varied]
    places = np.arange(256).reshape(sizes).transpose(fixed + list(varied))
    return places.reshape(-1, math.prod(sizes[d] for d in varied)).tolist()


SHARE_GROUPS = groups_of((0, 2))
OTHER_GROUPS = groups_of((1, 3))
def swap(parts, groups):
    return lax.all_to_all(parts, ("box", "depth"), 0, 0, axis_index_groups=groups, tiled=True)


def in_members(tiles):
    return tiles.reshape(MEMBERS, TILES // MEMBERS, 8, 128)


VISIBLE = pl.BlockSpec(memory_space=pltpu.VMEM)
REMOTE = pl.BlockSpec(memory_space=pl.ANY)
SUMS = (
    7,
    tuple(pltpu.HBM(shape, F32) for shape in ((X, TALL, Z), (X, TALL, Z), (X, Y, Z), (X, Y, Z), (TILES, 8, 128))),
    [
        ((X, Y, Z), F32), ((X, Y, Z), F32), ((3, Y * 16, 128), F32), ((256, 256), F32),
        ((NF, X, Y, Z), F32), ((3, X, Y, Z), F32), ((X, Y, Z), jnp.int32),
        ((X, TALL, Z), F32), ((X, TALL, Z), F32), ((X, Y, Z), F32), ((X, Y, Z), F32), ((TILES, 8, 128), F32),
        pltpu.SemaphoreType.DMA((5, 2)), pltpu.SemaphoreType.DMA((4, 4)),
    ],
    dict(in_specs=[REMOTE] * 3, out_specs=(REMOTE,) * 5, megabytes=58),
)
PACK_X = (
    2,
    (f32_like(PLANES, Y, Z), f32_like(PLANES, Y, Z)),
    [((2, PLANES - CSW, Y, Z), F32), pltpu.SemaphoreType.DMA((2, 7))],
    dict(in_specs=[REMOTE] * 4 + [VISIBLE] * 2, out_specs=(REMOTE, REMOTE), megabytes=20),
)
STEP = (
    14,
    (f32_like(NF, X, Y, Z), pltpu.HBM((X + 2, TALL, Z), F32), f32_like(TILES, 8, 128)),
    [
        ((X, Y, Z), F32), ((X, Y, Z), F32), ((4, Y, Z), F32), ((4, NF, Y, Z), F32), ((256, 256), BF16),
        ((X, 3, 64, 128), F32), ((NF, X + 2, TALL, Z), F32), ((3, Y * 16, 128), F32), ((256, 256), F32),
        ((NF, X, Y, Z), F32), ((X + 2, TALL, Z), F32), pltpu.SemaphoreType.DMA((X + 1,)),
    ],
    dict(out_specs=(REMOTE, REMOTE, VISIBLE), megabytes=24),
)
RING = (
    8,
    (f32_like(14, TALL, Z), f32_like(16, TALL, Z)),
    [
        ((16, TALL, Z), F32), ((14, TALL, Z), F32), ((16, TALL, Z), F32), ((3, 14, TALL, Z), F32), ((4, 12, TALL, Z), F32), ((TILES, 128), F32),
        pltpu.SemaphoreType.DMA((10,)), pltpu.SemaphoreType.DMA((3, 3)), pltpu.SemaphoreType.DMA((2,)),
    ],
    dict(in_specs=[VISIBLE] + [REMOTE] * 7, out_specs=(REMOTE, REMOTE), megabytes=58),
)
RELAX = (
    9,
    (pltpu.HBM((X, Y, Z), F32), pltpu.HBM((NF, NBINS), F32)),
    [
        ((14, TALL, Z), F32), ((16, TALL, Z), F32), ((2, 14, TALL, Z), F32), ((TILES, 128), F32),
        ((TILES, 8, 128), F32), ((TILES, 8, 128), F32), ((X, Y, Z), F32), ((NF, NBINS), F32),
        pltpu.SemaphoreType.DMA((5, 2)), pltpu.SemaphoreType.DMA((2,)),
    ],
    dict(in_specs=[REMOTE] * 4, out_specs=(REMOTE, REMOTE), megabytes=58),
)


MERGE = (0, (f32_like(2, 8, 128), f32_like(MEMBERS, 2, 8, 128)), [], dict(megabytes=20))


def per_device(state, velocity, bins):
    to_mate, to_next, weighted, shifted, tiles = call(sums_kernel, SUMS, state, velocity, bins)
    ymate, ynext = exchange(to_mate, to_next, "box")
    to_mate, to_next = call(pack_x_kernel, PACK_X, state, velocity, weighted, shifted, ymate, ynext)
    xmate, xnext = exchange(to_mate, to_next, "depth")
    share, copies = call(merge_kernel, MERGE, swap(in_members(tiles), SHARE_GROUPS))
    share, copies = call(divide_own_kernel, MERGE, swap(copies, OTHER_GROUPS))
    first = swap(copies, SHARE_GROUPS).reshape(TILES, 8, 128)
    new_state, near_p, tiles = call(step_kernel, STEP, first, state, velocity, bins, ymate, ynext, xmate, xnext)
    q, wide_bins = call(ring_kernel, RING, first, near_p, shifted, velocity, ymate, ynext, xmate, xnext)
    part, copies = call(merge_kernel, MERGE, swap(in_members(tiles), SHARE_GROUPS))
    copies, q, wide_bins = lax.optimization_barrier((copies, q, wide_bins))
    part, copies = call(divide_kernel, MERGE, swap(copies, OTHER_GROUPS), share)
    second = swap(copies, SHARE_GROUPS).reshape(TILES, 8, 128)
    potential, profile = call(relax_kernel, RELAX, second, first, q, wide_bins)
    return (new_state, potential, profile)


def solution(mesh):
    return jax.shard_map(
        per_device,
        mesh=mesh,
        in_specs=(
            P(None, "depth", "box", None),
            P(None, "depth", "box", None),
            P("depth", "box", None),
        ),
        out_specs=(P(None, "depth", "box", None), P("depth", "box", None), P()),
        check_vma=False,
    )
```

```python
import functools
import math

import jax
import jax.numpy as jnp
import numpy as np
from jax import lax
from jax.experimental import pallas as pl
from jax.experimental.pallas import tpu as pltpu
from jax.sharding import PartitionSpec as P

NBINS = 4096
COURANT = 0.8
OMEGA_RELAX = 0.8
DIAGONAL = 6.1
WEIGHTS = (1.0, 0.5, -0.5, 0.25, 0.75)
NF = 5
X, Y, Z = 8, 8, 384
TILES = NBINS // 128
SW, BN, VE, CSW, CBN, CVE, PLANES = 5, 9, 13, 22, 25, 28, 34
TALL = 24
MEMBERS = 16
F32, BF16 = jnp.float32, jnp.bfloat16


def pieces_of(values):
    upper = values.astype(BF16).astype(F32)
    rest = values - upper
    middle = rest.astype(BF16).astype(F32)
    return upper, middle, rest - middle


def lo_table(lo_row):
    wide = jnp.broadcast_to(lo_row, (16, Z)).astype(BF16)
    row = lax.broadcasted_iota(jnp.int32, (16, Z), 0).astype(F32).astype(BF16)
    one, zero = jnp.ones((16, Z), BF16), jnp.zeros((16, Z), BF16)
    return jnp.concatenate([jnp.where(wide == row + jnp.asarray(16 * k, BF16), one, zero) for k in range(16)], axis=0)


def hi_rows(hi_row, rows16):
    wide = jnp.broadcast_to(hi_row, (16, Z)).astype(BF16)
    zero = jnp.zeros((16, Z), BF16)
    return jnp.concatenate([jnp.where(wide == jnp.asarray(k, BF16), rows16, zero) for k in range(16)], axis=0)


def put_rows(rows, p, values):
    for j in range(3):
        rows[j, pl.ds(p, Y, stride=16), :] = values[:, j * 128 : (j + 1) * 128]


def get_rows(rows, y):
    return jnp.concatenate([rows[j, pl.ds(16 * y, 16), :].astype(BF16) for j in range(3)], axis=1)


def get_field(lifted, x, f):
    return jnp.concatenate([lifted[x, j, pl.ds(f, Y, stride=8), :] for j in range(3)], axis=1)


def add_bins(acc, rows, hi, lo, x):
    left, right = [], []
    for y in range(Y):
        left.append(hi_rows(hi[x, pl.ds(y, 1), :], get_rows(rows, y)))
        right.append(lo_table(lo[x, pl.ds(y, 1), :]))
    acc[...] += lax.dot_general(
        jnp.concatenate(left, 1), jnp.concatenate(right, 1), (((1,), (1,)), ((), ())), preferred_element_type=F32
    )


def put_sums(out, acc, extra):
    for k in range(16):
        s = acc[pl.ds(16 * k, 16), :]
        tile = jnp.concatenate([s[0:5] + s[5:10] + s[10:15], s[15:16], extra], axis=0)
        out[2 * k] = tile[:, :128]
        out[2 * k + 1] = tile[:, 128:]


def split_bins(bins, hi, lo):
    b = bins[...]
    hi[...] = lax.shift_right_logical(b, 8).astype(F32)
    lo[...] = (b & 255).astype(F32)


def is_odd(axis):
    return lax.rem(lax.axis_index(axis), 2) == 1


def start_by(odd, make, even_place, odd_place):
    @pl.when(jnp.logical_not(odd))
    def _():
        for copy in make(even_place, odd_place):
            copy.start()

    @pl.when(odd)
    def _():
        for copy in make(odd_place, even_place):
            copy.start()


def sums_kernel(
    state_in, velocity_in, bins_in, mate_out, next_out, weighted_out, shifted_out, tiles_out,
    hi, lo, rows, acc, state, velocity, bins, to_above, to_below, weighted, shifted, out, sems, out_sems
):
    bins_copy = pltpu.make_async_copy(bins_in, bins, sems.at[4, 0])
    bins_copy.start()

    def arrive(h):
        at = pl.ds(2 * h, 2)
        return [
            pltpu.make_async_copy(state_in.at[:, at], state.at[:, at], sems.at[h, 0]),
            pltpu.make_async_copy(velocity_in.at[:, at], velocity.at[:, at], sems.at[h, 1]),
        ]

    def leave(h, above_out, below_out):
        at = pl.ds(2 * h, 2)
        pairs = ((to_above, above_out), (to_below, below_out), (weighted, weighted_out), (shifted, shifted_out))
        return [pltpu.make_async_copy(src.at[at], dst.at[at], out_sems.at[h, i]) for i, (src, dst) in enumerate(pairs)]

    for h in range(4):
        for copy in arrive(h):
            copy.start()
    acc[...] = jnp.zeros_like(acc)
    put_rows(rows, 15, jnp.ones((Y, Z), F32))
    bins_copy.wait()
    split_bins(bins, hi, lo)
    shifted[...] = bins[...].astype(F32) + 1.0

    def step(x, top):
        s = [state[f, x] for f in range(NF)]
        w = WEIGHTS[0] * s[0]
        for f in range(NF):
            for i, piece in enumerate(pieces_of(s[f])):
                put_rows(rows, NF * i + f, piece)
            if f > 0:
                w += WEIGHTS[f] * s[f]
        add_bins(acc, rows, hi, lo, x)
        weighted[x] = w
        b = shifted[x]
        v = [velocity[d, x] for d in range(3)]
        for face, near, four, three in ((to_above, Y - 1, Y - 4, Y - 3), (to_below, 0, 0, 0)):
            parts = [c[near : near + 1] for c in s] + [w[four : four + 4], b[four : four + 4]]
            parts += [c[three : three + 3] for c in v] + [jnp.zeros((2, Z), F32)]
            face[x] = jnp.concatenate(parts, axis=0)
        return jnp.maximum(top, jnp.abs(v[0]) + jnp.abs(v[1]) + jnp.abs(v[2]))

    top = jnp.zeros((Y, Z), F32)
    def two(h, top):
        for copy in arrive(h):
            copy.wait()
        top = step(2 * h + 1, step(2 * h, top))
        start_by(is_odd("box"), functools.partial(leave, h), mate_out, next_out)
        return top

    top = lax.fori_loop(0, 4, two, top)
    put_sums(out, acc, jnp.full((2, 256), jnp.max(top), F32))
    tiles_copy = pltpu.make_async_copy(out, tiles_out, sems.at[4, 1])
    tiles_copy.start()
    tiles_copy.wait()
    for h in range(4):
        for copy in leave(h, mate_out, next_out):
            copy.wait()


def pack_x_kernel(state, velocity, weighted, shifted, ymate, ynext, mate_out, next_out, corners, sems):
    def fill(to_above, to_below):
        copies = []
        for side, (out, near, four, three) in enumerate(((to_above, X - 1, X - 4, X - 3), (to_below, 0, 0, 0))):
            parts = [(state.at[:, near], 0, NF), (weighted.at[pl.ds(four, 4)], SW, 4), (shifted.at[pl.ds(four, 4)], BN, 4)]
            parts += [(velocity.at[d, pl.ds(three, 3)], VE + 3 * d, 3) for d in range(3)]
            for i, (src, at, n) in enumerate(parts):
                copies.append(pltpu.make_async_copy(src, out.at[pl.ds(at, n)], sems.at[side, i]))
        return copies

    def fill_corners(to_above, to_below):
        return [
            pltpu.make_async_copy(corners.at[side], out.at[pl.ds(CSW, PLANES - CSW)], sems.at[side, 6])
            for side, out in enumerate((to_above, to_below))
        ]

    start_by(is_odd("depth"), fill, mate_out, next_out)
    odd = is_odd("box")
    gap = jnp.zeros((1, Z), F32)
    for side, (three, two) in enumerate(((X - 3, X - 2), (0, 0))):
        for x in range(three, three + 3):
            ylo, yhi = jnp.where(odd, ymate[x], ynext[x]), jnp.where(odd, ynext[x], ymate[x])
            for at, row in ((CSW, SW), (CBN, BN)):
                corners[side, at - CSW + x - three] = jnp.concatenate([ylo[row : row + 4], yhi[row : row + 4]], axis=0)
            if 0 <= x - two < 2:
                for d in range(3):
                    row = VE + 3 * d
                    corners[side, CVE - CSW + 2 * d + x - two] = jnp.concatenate(
                        [ylo[row : row + 3], gap, yhi[row : row + 3], gap], axis=0
                    )
    start_by(is_odd("depth"), fill_corners, mate_out, next_out)
    for copy in fill(mate_out, next_out) + fill_corners(mate_out, next_out):
        copy.wait()


def lift_row(table, hi_row, lo_row):
    found = lax.dot_general(table, lo_table(lo_row), (((1,), (0,)), ((), ())), preferred_element_type=F32)
    wide = jnp.broadcast_to(hi_row, (16, Z))
    acc = jnp.zeros((16, Z), F32)
    for k in range(16):
        acc = jnp.where(wide == float(k), found[16 * k : 16 * k + 16], acc)
    total = acc[0:5] + acc[5:10] + acc[10:15]
    return jnp.concatenate([total, jnp.zeros((3, Z), F32)], axis=0)


def lift_five(first, b):
    index = b.astype(jnp.int32)
    parts = [[] for f in range(NF)]
    for j in range(3):
        cut = index[:, 128 * j : 128 * j + 128]
        tile, lane = lax.shift_right_arithmetic(cut, 7), cut & 127
        found = [jnp.zeros((8, 128), F32)] * NF
        for t in range(TILES):
            here = tile == t
            for f in range(NF):
                row = jnp.broadcast_to(first[t, f : f + 1, :], (8, 128))
                found[f] = jnp.where(here, jnp.take_along_axis(row, lane, axis=1), found[f])
        for f in range(NF):
            parts[f].append(found[f])
    return [jnp.concatenate(part, axis=1) for part in parts]


def step_kernel(
    first, state, velocity, bins, ymate, ynext, xmate, xnext, new_state_out, near_out, out,
    hi, lo, face_bins, face_lift, table, lifted, p, rows, acc, new_state, near_p, sems
):
    for k in range(16):
        pair = jnp.concatenate([first[2 * k], first[2 * k + 1]], axis=1)
        u, m, l = pieces_of(pair)
        block = jnp.concatenate([u[0:5], m[0:5], l[0:5], jnp.zeros((1, 256), F32)], axis=0)
        table[pl.ds(16 * k, 16), :] = block.astype(BF16)
    tab = table[...]
    time_step = COURANT / (1.0 + jnp.max(first[0, 6:7, :]))
    split_bins(bins, hi, lo)
    odd_y, odd_x = is_odd("box"), is_odd("depth")

    def lower(odd, mate, other):
        return jnp.where(odd, mate, other)

    def upper(odd, mate, other):
        return jnp.where(odd, other, mate)

    for x in range(X):
        face_bins[0, x : x + 1, :] = lower(odd_y, ymate[x, BN + 3 : BN + 4, :], ynext[x, BN + 3 : BN + 4, :]) - 1.0
        face_bins[1, x : x + 1, :] = upper(odd_y, ymate[x, BN : BN + 1, :], ynext[x, BN : BN + 1, :]) - 1.0
    face_bins[2] = lower(odd_x, xmate[BN + 3], xnext[BN + 3]) - 1.0
    face_bins[3] = upper(odd_x, xmate[BN], xnext[BN]) - 1.0

    def lift_some(i, carry):
        for k in range(2):
            x = 2 * i + k
            for y in range(Y):
                eight = lift_row(tab, hi[x, pl.ds(y, 1), :], lo[x, pl.ds(y, 1), :])
                for j in range(3):
                    lifted[x, j, pl.ds(8 * y, 8), :] = eight[:, 128 * j : 128 * j + 128]
        for f, value in enumerate(lift_five(first, face_bins[i])):
            face_lift[i, f] = value
        for k in range(2):
            x = 2 * i + k
            for f in range(NF):
                p[f, x + 1, pl.ds(8, 8), :] = state[f, x] - get_field(lifted, x, f)
        return carry

    for i in range(4):
        lift_some(i, 0)
    for f in range(NF):
        p[f, 0, pl.ds(8, 8), :] = lower(odd_x, xmate[f], xnext[f]) - face_lift[2, f]
        p[f, X + 1, pl.ds(8, 8), :] = upper(odd_x, xmate[f], xnext[f]) - face_lift[3, f]
        for x in range(X):
            mate, other = ymate[x, f : f + 1, :], ynext[x, f : f + 1, :]
            p[f, x + 1, 7:8, :] = lower(odd_y, mate, other) - face_lift[0, f, x : x + 1, :]
            p[f, x + 1, 16:17, :] = upper(odd_y, mate, other) - face_lift[1, f, x : x + 1, :]

    acc[...] = jnp.zeros_like(acc)
    lane = lax.broadcasted_iota(jnp.int32, (Y, Z), 1)
    put_rows(rows, 15, jnp.zeros((Y, Z), F32))

    def advect(x, carry):
        v = [velocity[d, x] for d in range(3)]
        up = [jnp.maximum(c, 0.0) for c in v]
        down = [jnp.minimum(c, 0.0) for c in v]
        for f in range(NF):
            c = p[f, x + 1, pl.ds(8, 8), :]
            before = jnp.where(lane == 0, 0.0, pltpu.roll(c, 1, 1))
            after = jnp.where(lane == Z - 1, 0.0, pltpu.roll(c, Z - 1, 1))
            change = up[0] * (c - p[f, x, pl.ds(8, 8), :]) + down[0] * (p[f, x + 2, pl.ds(8, 8), :] - c)
            change += up[1] * (c - p[f, x + 1, pl.ds(7, 8), :]) + down[1] * (p[f, x + 1, pl.ds(9, 8), :] - c)
            change += up[2] * (c - before) + down[2] * (after - c)
            moved = c - time_step * change
            new_state[f, x] = get_field(lifted, x, f) + moved
            for i, piece in enumerate(pieces_of(moved)):
                put_rows(rows, NF * i + f, piece)
        state_copy(x).start()
        add_bins(acc, rows, hi, lo, x)
        return carry

    def state_copy(x):
        return pltpu.make_async_copy(new_state.at[:, x], new_state_out.at[:, x], sems.at[x])


    for x in range(X + 2):
        total = WEIGHTS[0] * p[0, x]
        for f in range(1, NF):
            total += WEIGHTS[f] * p[f, x]
        near_p[x] = total
    near_copy = pltpu.make_async_copy(near_p, near_out, sems.at[X])
    near_copy.start()
    lax.fori_loop(0, X // 2, lambda i, c: advect(2 * i + 1, advect(2 * i, c)), 0)
    put_sums(out, acc, jnp.zeros((2, 256), F32))
    for x in range(X):
        state_copy(x).wait()
    near_copy.wait()


def weighted_rows(tiles):
    total = jnp.zeros((TILES, 128), F32)
    for f in range(NF):
        total += WEIGHTS[f] * tiles[:, f, :]
    return total


def row_table(total, pieces):
    return jnp.concatenate(pieces_of(total)[:pieces], axis=0).astype(BF16)


def lift_one(tab, b):
    high = jnp.floor(b * (1.0 / 128.0))
    low = b - 128.0 * high
    row = lax.broadcasted_iota(jnp.int32, (TILES, Z), 0).astype(F32)
    row16 = lax.broadcasted_iota(jnp.int32, (16, Z), 0).astype(F32).astype(BF16)
    one, zero = jnp.ones((16, Z), BF16), jnp.zeros((16, Z), BF16)
    wide = jnp.broadcast_to(low, (16, Z)).astype(BF16)
    t = jnp.concatenate([jnp.where(wide == row16 + jnp.asarray(16 * k, BF16), one, zero) for k in range(8)], axis=0)
    found = lax.dot_general(tab, t, (((1,), (0,)), ((), ())), preferred_element_type=F32)
    total = found[0:TILES]
    for i in range(1, tab.shape[0] // TILES):
        total += found[TILES * i : TILES * i + TILES]
    return jnp.sum(jnp.where(jnp.broadcast_to(high, (TILES, Z)) == row, total, 0.0), axis=0, keepdims=True)


def lift_eight(table, b):
    index = b.astype(jnp.int32)
    parts = []
    for j in range(3):
        cut = index[:, 128 * j : 128 * j + 128]
        tile, lane = lax.shift_right_arithmetic(cut, 7), cut & 127
        found = jnp.zeros((8, 128), F32)
        for t in range(TILES):
            row = jnp.broadcast_to(table[t : t + 1, :], (8, 128))
            found = jnp.where(tile == t, jnp.take_along_axis(row, lane, axis=1), found)
        parts.append(found)
    return jnp.concatenate(parts, axis=1)


def reach_rows(far):
    near = {0: range(7, 17), 1: range(8, 16)}
    return {d: [y for y in range(8 - far + d, 16 + far - d) if y not in near.get(d, ())] for d in range(far + 1)}


def ring_kernel(
    first, near_p, shifted, velocity, ymate, ynext, xmate, xnext, q_out, bins_out, p, q, high, v, faces, flat, sems, v_sems, out_sems
):
    def own():
        return [
            pltpu.make_async_copy(near_p, p.at[pl.ds(3, 10)], sems.at[0]),
            pltpu.make_async_copy(shifted, high.at[pl.ds(4, 8), pl.ds(8, 8)], sems.at[1]),
        ]

    def along_y(yhi, ylo):
        return [
            pltpu.make_async_copy(ylo, faces.at[0, pl.ds(0, 8)], sems.at[2]),
            pltpu.make_async_copy(yhi, faces.at[1, pl.ds(0, 8)], sems.at[3]),
        ]

    def along_x(xhi, xlo):
        blocks = [
            (xlo.at[pl.ds(SW, 3)], p.at[pl.ds(0, 3), pl.ds(8, 8)]),
            (xhi.at[pl.ds(SW + 1, 3)], p.at[pl.ds(13, 3), pl.ds(8, 8)]),
            (xlo.at[pl.ds(BN, 4)], high.at[pl.ds(0, 4), pl.ds(8, 8)]),
            (xhi.at[pl.ds(BN, 4)], high.at[pl.ds(12, 4), pl.ds(8, 8)]),
            (xlo.at[pl.ds(CSW, 12)], faces.at[2, pl.ds(0, 12), pl.ds(0, 8)]),
            (xhi.at[pl.ds(CSW, 12)], faces.at[3, pl.ds(0, 12), pl.ds(0, 8)]),
        ]
        return [pltpu.make_async_copy(src, dst, sems.at[4 + i]) for i, (src, dst) in enumerate(blocks)]

    def own_speed():
        return [pltpu.make_async_copy(velocity.at[d], v.at[d, pl.ds(3, 8), pl.ds(8, 8)], v_sems.at[d, 0]) for d in range(3)]

    def speed_x(xhi, xlo):
        copies = []
        for d in range(3):
            for i, (src, at) in enumerate(((xlo, 0), (xhi, 11))):
                src = src.at[pl.ds(VE + 3 * d, 3)]
                copies.append(pltpu.make_async_copy(src, v.at[d, pl.ds(at, 3), pl.ds(8, 8)], v_sems.at[d, 1 + i]))
        return copies

    for copy in own():
        copy.start()
    start_by(is_odd("box"), along_y, ymate, ynext)
    start_by(is_odd("depth"), along_x, xmate, xnext)
    for copy in own_speed():
        copy.start()
    start_by(is_odd("depth"), speed_x, xmate, xnext)
    early = own() + along_y(ymate, ynext) + along_x(xmate, xnext)
    late = own_speed() + speed_x(xmate, xnext)
    flat[...] = weighted_rows(first)
    tab = row_table(flat[...], 3)
    for copy in early:
        copy.wait()
    below, above, left, right = (faces.at[i] for i in range(4))
    p[pl.ds(4, 8), 4:7, :] = below[0:8, SW : SW + 3, :]
    p[pl.ds(4, 8), 17:20, :] = above[0:8, SW + 1 : SW + 4, :]
    high[pl.ds(4, 8), 4:8, :] = below[0:8, BN : BN + 4, :]
    high[pl.ds(4, 8), 16:20, :] = above[0:8, BN : BN + 4, :]
    for dst, corner in ((p, 0), (high, CBN - CSW)):
        for ref, at in ((left, 1), (right, 12)):
            dst[pl.ds(at, 3), 4:8, :] = ref[pl.ds(corner, 3), 0:4, :]
            dst[pl.ds(at, 3), 16:20, :] = ref[pl.ds(corner, 3), 4:8, :]
    bins_copy = pltpu.make_async_copy(high, bins_out, out_sems.at[0])
    bins_copy.start()
    rows = reach_rows(4)

    def lift_x(x, rows, block):
        if block:
            p[x, 8:16, :] = p[x, 8:16, :] - lift_eight(flat, high[x, 8:16, :] - 1.0)
        for y in rows:
            p[x, y : y + 1, :] = p[x, y : y + 1, :] - lift_one(tab, high[x, y : y + 1, :] - 1.0)

    def lift_sides(side, carry):
        for d in range(2, 5):
            lift_x((4 - d) + side * (7 + 2 * d), [y for y in rows[d] if not 8 <= y < 16], True)
        lift_x(3 + side * 9, rows[1], False)
        for i in range(4):
            lift_x(4 + 4 * side + i, rows[0], False)
        return carry

    for side in range(2):
        lift_sides(side, 0)
    for copy in late:
        copy.wait()
    for d in range(3):
        row, corner = VE + 3 * d, CVE - CSW + 2 * d
        v[d, pl.ds(3, 8), 5:8, :] = below[0:8, row : row + 3, :]
        v[d, pl.ds(3, 8), 16:19, :] = above[0:8, row : row + 3, :]
        for ref, at in ((left, 1), (right, 11)):
            v[d, pl.ds(at, 2), 5:8, :] = ref[pl.ds(corner, 2), 0:3, :]
            v[d, pl.ds(at, 2), 16:19, :] = ref[pl.ds(corner, 2), 4:7, :]
    time_step = COURANT / (1.0 + jnp.max(first[0, 6:7, :]))
    lane = lax.broadcasted_iota(jnp.int32, (TALL, Z), 1)

    for x in range(14):
        c = p[x + 1]
        sides = (
            (p[x], p[x + 2]),
            (pltpu.roll(c, 1, 0), pltpu.roll(c, TALL - 1, 0)),
            (jnp.where(lane == 0, 0.0, pltpu.roll(c, 1, 1)), jnp.where(lane == Z - 1, 0.0, pltpu.roll(c, Z - 1, 1))),
        )
        change = jnp.zeros((TALL, Z), F32)
        for d, (before, after) in enumerate(sides):
            change += jnp.maximum(v[d, x], 0.0) * (c - before) + jnp.minimum(v[d, x], 0.0) * (after - c)
        q[x] = c - time_step * change
    q_copy = pltpu.make_async_copy(q, q_out, out_sems.at[1])
    q_copy.start()
    q_copy.wait()
    bins_copy.wait()


def relax_kernel(
    second_in, first_in, q_in, bins_in, potential_out, profile_out, src, high, pot, flat, second, first, potential, profile, sems, out_sems
):
    tables = [
        pltpu.make_async_copy(second_in, second, sems.at[4, 0]),
        pltpu.make_async_copy(first_in, first, sems.at[4, 1]),
    ]
    blocks = []
    for at, n in ((3, 4), (7, 4), (0, 3), (11, 3)):
        bins_at = pl.ds(at + 1, n)
        at = pl.ds(at, n)
        i = len(blocks)
        blocks.append([
            pltpu.make_async_copy(q_in.at[at], src.at[at], sems.at[i, 0]),
            pltpu.make_async_copy(bins_in.at[bins_at], high.at[bins_at], sems.at[i, 1]),
        ])
    for pair in [tables] + blocks:
        for copy in pair:
            copy.start()
    for copy in tables:
        copy.wait()
    for t in range(TILES):
        second[t] = second[t] / jnp.maximum(first[t, 5:6, :], 1.0)
    flat[...] = weighted_rows(second)
    tab = row_table(flat[...], 2)
    for t in range(TILES):
        profile[:, 128 * t : 128 * t + 128] = (first[t] + second[t])[0:NF]
    profile_copy = pltpu.make_async_copy(profile, profile_out, out_sems.at[0])
    profile_copy.start()

    def lift_x(x, rows, block):
        if block:
            src[x, 8:16, :] = src[x, 8:16, :] - lift_eight(flat, high[x + 1, 8:16, :] - 1.0)
        for y in rows:
            src[x, y : y + 1, :] = src[x, y : y + 1, :] - lift_one(tab, high[x + 1, y : y + 1, :] - 1.0)
        scaled = src[x] * (OMEGA_RELAX / DIAGONAL)
        src[x] = scaled
        pot[0, x] = scaled

    def lift_sides(side, carry):
        for d in range(1, 4):
            rows = [y for y in range(5 + d, 19 - d) if d == 3 or not 8 <= y < 16]
            lift_x((3 - d) + side * (7 + 2 * d), rows, d < 3)
        return carry

    for h in range(2):
        for copy in blocks[h]:
            copy.wait()
        for x in range(3 + 4 * h, 7 + 4 * h):
            lift_x(x, (5, 6, 7, 16, 17, 18), True)
    for pair in blocks[2:]:
        for copy in pair:
            copy.wait()
    for side in range(2):
        lift_sides(side, 0)
    lane = lax.broadcasted_iota(jnp.int32, (TALL, Z), 1)
    for s in range(1, 4):
        now, later = (s + 1) % 2, s % 2
        for x in range(s, 14 - s):
            c = pot[now, x]
            near = pot[now, x - 1] + pot[now, x + 1]
            near += pltpu.roll(c, 1, 0) + pltpu.roll(c, TALL - 1, 0)
            near += jnp.where(lane == 0, 0.0, pltpu.roll(c, 1, 1)) + jnp.where(lane == Z - 1, 0.0, pltpu.roll(c, Z - 1, 1))
            new = (1.0 - OMEGA_RELAX) * c + (src[x] + (OMEGA_RELAX / DIAGONAL) * near)
            if s < 3:
                pot[later, x] = jnp.where(high[x + 1] < 0.5, 0.0, new)
            else:
                potential[x - 3] = new[8:16]
    potential_copy = pltpu.make_async_copy(potential, potential_out, out_sems.at[1])
    potential_copy.start()
    potential_copy.wait()
    profile_copy.wait()


def f32_like(*shape):
    return jax.ShapeDtypeStruct(shape, F32)


def call(kernel, plan, *args):
    micros, out_shape, scratch, more = plan
    more = dict(more)
    limit = more.pop("megabytes") * 1024 * 1024
    return pl.pallas_call(
        kernel,
        out_shape=out_shape,
        cost_estimate=pl.CostEstimate(flops=micros * 1_000_000_000, bytes_accessed=0, transcendentals=0),
        scratch_shapes=[pltpu.VMEM(*part) if isinstance(part, tuple) else part for part in scratch],
        compiler_params=pltpu.CompilerParams(vmem_limit_bytes=limit),
        **more,
    )(*args)


def exchange(to_mate, to_next, axis):
    count = lax.axis_size(axis)
    mates = [(i, i ^ 1) for i in range(count)]
    others = [pair for i in range(1, count - 1, 2) for pair in ((i, i + 1), (i + 1, i))]
    return lax.ppermute(to_mate, axis, mates), lax.ppermute(to_next, axis, others)


def added(tiles):
    total, top = tiles[0], tiles[0]
    for i in range(1, tiles.shape[0]):
        total, top = total + tiles[i], jnp.maximum(top, tiles[i])
    return jnp.where(lax.broadcasted_iota(jnp.int32, total.shape, total.ndim - 2) == 6, top, total)


def merge_kernel(tiles, copies):
    total = added(tiles)
    for i in range(copies.shape[0]):
        copies[i] = total


def divide_kernel(tiles, copies):
    total = added(tiles)
    row = lax.broadcasted_iota(jnp.int32, total.shape, 1)
    mean = jnp.where(row < NF, total / jnp.maximum(total[:, 5:6, :], 1.0), total)
    for i in range(MEMBERS):
        copies[i] = mean


def groups_of(varied):
    sizes = (4, 8, 4, 2)
    fixed = [d for d in range(4) if d not in varied]
    places = np.arange(256).reshape(sizes).transpose(fixed + list(varied))
    return places.reshape(-1, math.prod(sizes[d] for d in varied)).tolist()


SHARE_GROUPS = groups_of((0, 2))
OTHER_GROUPS = groups_of((1, 3))
LAYER_GROUPS = groups_of((0, 2, 3))
COLUMN_GROUPS = groups_of((1,))
def swap(parts, groups):
    return lax.all_to_all(parts, ("box", "depth"), 0, 0, axis_index_groups=groups, tiled=True)


def in_members(tiles):
    return tiles.reshape(MEMBERS, TILES // MEMBERS, 8, 128)


VISIBLE = pl.BlockSpec(memory_space=pltpu.VMEM)
REMOTE = pl.BlockSpec(memory_space=pl.ANY)
SUMS = (
    7,
    tuple(pltpu.HBM(shape, F32) for shape in ((X, TALL, Z), (X, TALL, Z), (X, Y, Z), (X, Y, Z), (TILES, 8, 128))),
    [
        ((X, Y, Z), F32), ((X, Y, Z), F32), ((3, Y * 16, 128), F32), ((256, 256), F32),
        ((NF, X, Y, Z), F32), ((3, X, Y, Z), F32), ((X, Y, Z), jnp.int32),
        ((X, TALL, Z), F32), ((X, TALL, Z), F32), ((X, Y, Z), F32), ((X, Y, Z), F32), ((TILES, 8, 128), F32),
        pltpu.SemaphoreType.DMA((5, 2)), pltpu.SemaphoreType.DMA((4, 4)),
    ],
    dict(in_specs=[REMOTE] * 3, out_specs=(REMOTE,) * 5, megabytes=58),
)
PACK_X = (
    2,
    (f32_like(PLANES, Y, Z), f32_like(PLANES, Y, Z)),
    [((2, PLANES - CSW, Y, Z), F32), pltpu.SemaphoreType.DMA((2, 7))],
    dict(in_specs=[REMOTE] * 4 + [VISIBLE] * 2, out_specs=(REMOTE, REMOTE), megabytes=20),
)
STEP = (
    14,
    (f32_like(NF, X, Y, Z), pltpu.HBM((X + 2, TALL, Z), F32), f32_like(TILES, 8, 128)),
    [
        ((X, Y, Z), F32), ((X, Y, Z), F32), ((4, Y, Z), F32), ((4, NF, Y, Z), F32), ((256, 256), BF16),
        ((X, 3, 64, 128), F32), ((NF, X + 2, TALL, Z), F32), ((3, Y * 16, 128), F32), ((256, 256), F32),
        ((NF, X, Y, Z), F32), ((X + 2, TALL, Z), F32), pltpu.SemaphoreType.DMA((X + 1,)),
    ],
    dict(out_specs=(REMOTE, REMOTE, VISIBLE), megabytes=24),
)
RING = (
    8,
    (f32_like(14, TALL, Z), f32_like(16, TALL, Z)),
    [
        ((16, TALL, Z), F32), ((14, TALL, Z), F32), ((16, TALL, Z), F32), ((3, 14, TALL, Z), F32), ((4, 12, TALL, Z), F32), ((TILES, 128), F32),
        pltpu.SemaphoreType.DMA((10,)), pltpu.SemaphoreType.DMA((3, 3)), pltpu.SemaphoreType.DMA((2,)),
    ],
    dict(in_specs=[VISIBLE] + [REMOTE] * 7, out_specs=(REMOTE, REMOTE), megabytes=58),
)
RELAX = (
    9,
    (pltpu.HBM((X, Y, Z), F32), pltpu.HBM((NF, NBINS), F32)),
    [
        ((14, TALL, Z), F32), ((16, TALL, Z), F32), ((2, 14, TALL, Z), F32), ((TILES, 128), F32),
        ((TILES, 8, 128), F32), ((TILES, 8, 128), F32), ((X, Y, Z), F32), ((NF, NBINS), F32),
        pltpu.SemaphoreType.DMA((5, 2)), pltpu.SemaphoreType.DMA((2,)),
    ],
    dict(in_specs=[REMOTE] * 4, out_specs=(REMOTE, REMOTE), megabytes=58),
)


MERGE = (0, f32_like(MEMBERS, 2, 8, 128), [], dict(megabytes=20))
COLUMN = (0, f32_like(8, 8, 128), [], dict(megabytes=20))
LAYER = (0, f32_like(TILES, 8, 128), [], dict(megabytes=20))


def per_device(state, velocity, bins):
    to_mate, to_next, weighted, shifted, tiles = call(sums_kernel, SUMS, state, velocity, bins)
    ymate, ynext = exchange(to_mate, to_next, "box")
    to_mate, to_next = call(pack_x_kernel, PACK_X, state, velocity, weighted, shifted, ymate, ynext)
    xmate, xnext = exchange(to_mate, to_next, "depth")
    copies = call(merge_kernel, MERGE, swap(in_members(tiles), SHARE_GROUPS))
    copies = call(divide_kernel, MERGE, swap(copies, OTHER_GROUPS))
    first = swap(copies, SHARE_GROUPS).reshape(TILES, 8, 128)
    new_state, near_p, tiles = call(step_kernel, STEP, first, state, velocity, bins, ymate, ynext, xmate, xnext)
    q, wide_bins = call(ring_kernel, RING, first, near_p, shifted, velocity, ymate, ynext, xmate, xnext)
    copies = call(merge_kernel, COLUMN, swap(tiles, LAYER_GROUPS))
    copies, q, wide_bins = lax.optimization_barrier((copies, q, wide_bins))
    copies = call(merge_kernel, LAYER, swap(copies, COLUMN_GROUPS))
    second = swap(copies, LAYER_GROUPS)
    potential, profile = call(relax_kernel, RELAX, second, first, q, wide_bins)
    return (new_state, potential, profile)


def solution(mesh):
    return jax.shard_map(
        per_device,
        mesh=mesh,
        in_specs=(
            P(None, "depth", "box", None),
            P(None, "depth", "box", None),
            P("depth", "box", None),
        ),
        out_specs=(P(None, "depth", "box", None), P("depth", "box", None), P()),
        check_vma=False,
    )
```

```python
import functools
import math

import jax
import jax.numpy as jnp
import numpy as np
from jax import lax
from jax.experimental import pallas as pl
from jax.experimental.pallas import tpu as pltpu
from jax.sharding import PartitionSpec as P

NBINS = 4096
COURANT = 0.8
OMEGA_RELAX = 0.8
DIAGONAL = 6.1
WEIGHTS = (1.0, 0.5, -0.5, 0.25, 0.75)
NF = 5
X, Y, Z = 8, 8, 384
TILES = NBINS // 128
SW, BN, VE, CSW, CBN, CVE, PLANES = 5, 9, 13, 22, 25, 28, 34
TALL = 24
MEMBERS = 16
F32, BF16 = jnp.float32, jnp.bfloat16


def pieces_of(values):
    upper = values.astype(BF16).astype(F32)
    rest = values - upper
    middle = rest.astype(BF16).astype(F32)
    return upper, middle, rest - middle


def lo_table(lo_row):
    wide = jnp.broadcast_to(lo_row, (16, Z)).astype(BF16)
    row = lax.broadcasted_iota(jnp.int32, (16, Z), 0).astype(F32).astype(BF16)
    one, zero = jnp.ones((16, Z), BF16), jnp.zeros((16, Z), BF16)
    return jnp.concatenate([jnp.where(wide == row + jnp.asarray(16 * k, BF16), one, zero) for k in range(16)], axis=0)


def hi_rows(hi_row, rows16):
    wide = jnp.broadcast_to(hi_row, (16, Z)).astype(BF16)
    zero = jnp.zeros((16, Z), BF16)
    return jnp.concatenate([jnp.where(wide == jnp.asarray(k, BF16), rows16, zero) for k in range(16)], axis=0)


def put_rows(rows, p, values):
    for j in range(3):
        rows[j, pl.ds(p, Y, stride=16), :] = values[:, j * 128 : (j + 1) * 128]


def get_rows(rows, y):
    return jnp.concatenate([rows[j, pl.ds(16 * y, 16), :].astype(BF16) for j in range(3)], axis=1)


def get_field(lifted, x, f):
    return jnp.concatenate([lifted[x, j, pl.ds(f, Y, stride=8), :] for j in range(3)], axis=1)


def add_bins(acc, rows, hi, lo, x):
    left, right = [], []
    for y in range(Y):
        left.append(hi_rows(hi[x, pl.ds(y, 1), :], get_rows(rows, y)))
        right.append(lo_table(lo[x, pl.ds(y, 1), :]))
    acc[...] += lax.dot_general(
        jnp.concatenate(left, 1), jnp.concatenate(right, 1), (((1,), (1,)), ((), ())), preferred_element_type=F32
    )


def put_sums(out, acc, extra):
    for k in range(16):
        s = acc[pl.ds(16 * k, 16), :]
        tile = jnp.concatenate([s[0:5] + s[5:10] + s[10:15], s[15:16], extra], axis=0)
        out[2 * k] = tile[:, :128]
        out[2 * k + 1] = tile[:, 128:]


def split_bins(bins, hi, lo):
    b = bins[...]
    hi[...] = lax.shift_right_logical(b, 8).astype(F32)
    lo[...] = (b & 255).astype(F32)


def is_odd(axis):
    return lax.rem(lax.axis_index(axis), 2) == 1


def start_by(odd, make, even_place, odd_place):
    @pl.when(jnp.logical_not(odd))
    def _():
        for copy in make(even_place, odd_place):
            copy.start()

    @pl.when(odd)
    def _():
        for copy in make(odd_place, even_place):
            copy.start()


def sums_kernel(
    state_in, velocity_in, bins_in, mate_out, next_out, weighted_out, shifted_out, tiles_out,
    hi, lo, rows, acc, state, velocity, bins, to_above, to_below, weighted, shifted, out, sems, out_sems
):
    bins_copy = pltpu.make_async_copy(bins_in, bins, sems.at[4, 0])
    bins_copy.start()

    def arrive(h):
        at = pl.ds(2 * h, 2)
        return [
            pltpu.make_async_copy(state_in.at[:, at], state.at[:, at], sems.at[h, 0]),
            pltpu.make_async_copy(velocity_in.at[:, at], velocity.at[:, at], sems.at[h, 1]),
        ]

    def leave(h, above_out, below_out):
        at = pl.ds(2 * h, 2)
        pairs = ((to_above, above_out), (to_below, below_out), (weighted, weighted_out), (shifted, shifted_out))
        return [pltpu.make_async_copy(src.at[at], dst.at[at], out_sems.at[h, i]) for i, (src, dst) in enumerate(pairs)]

    for h in range(4):
        for copy in arrive(h):
            copy.start()
    acc[...] = jnp.zeros_like(acc)
    put_rows(rows, 15, jnp.ones((Y, Z), F32))
    bins_copy.wait()
    split_bins(bins, hi, lo)
    shifted[...] = bins[...].astype(F32) + 1.0

    def step(x, top):
        s = [state[f, x] for f in range(NF)]
        w = WEIGHTS[0] * s[0]
        for f in range(NF):
            for i, piece in enumerate(pieces_of(s[f])):
                put_rows(rows, NF * i + f, piece)
            if f > 0:
                w += WEIGHTS[f] * s[f]
        add_bins(acc, rows, hi, lo, x)
        weighted[x] = w
        b = shifted[x]
        v = [velocity[d, x] for d in range(3)]
        for face, near, four, three in ((to_above, Y - 1, Y - 4, Y - 3), (to_below, 0, 0, 0)):
            parts = [c[near : near + 1] for c in s] + [w[four : four + 4], b[four : four + 4]]
            parts += [c[three : three + 3] for c in v] + [jnp.zeros((2, Z), F32)]
            face[x] = jnp.concatenate(parts, axis=0)
        return jnp.maximum(top, jnp.abs(v[0]) + jnp.abs(v[1]) + jnp.abs(v[2]))

    top = jnp.zeros((Y, Z), F32)
    def two(h, top):
        for copy in arrive(h):
            copy.wait()
        top = step(2 * h + 1, step(2 * h, top))
        start_by(is_odd("box"), functools.partial(leave, h), mate_out, next_out)
        return top

    top = lax.fori_loop(0, 4, two, top)
    put_sums(out, acc, jnp.full((2, 256), jnp.max(top), F32))
    tiles_copy = pltpu.make_async_copy(out, tiles_out, sems.at[4, 1])
    tiles_copy.start()
    tiles_copy.wait()
    for h in range(4):
        for copy in leave(h, mate_out, next_out):
            copy.wait()


def pack_x_kernel(state, velocity, weighted, shifted, ymate, ynext, mate_out, next_out, corners, sems):
    def fill(to_above, to_below):
        copies = []
        for side, (out, near, four, three) in enumerate(((to_above, X - 1, X - 4, X - 3), (to_below, 0, 0, 0))):
            parts = [(state.at[:, near], 0, NF), (weighted.at[pl.ds(four, 4)], SW, 4), (shifted.at[pl.ds(four, 4)], BN, 4)]
            parts += [(velocity.at[d, pl.ds(three, 3)], VE + 3 * d, 3) for d in range(3)]
            for i, (src, at, n) in enumerate(parts):
                copies.append(pltpu.make_async_copy(src, out.at[pl.ds(at, n)], sems.at[side, i]))
        return copies

    def fill_corners(to_above, to_below):
        return [
            pltpu.make_async_copy(corners.at[side], out.at[pl.ds(CSW, PLANES - CSW)], sems.at[side, 6])
            for side, out in enumerate((to_above, to_below))
        ]

    start_by(is_odd("depth"), fill, mate_out, next_out)
    odd = is_odd("box")
    gap = jnp.zeros((1, Z), F32)
    for side, (three, two) in enumerate(((X - 3, X - 2), (0, 0))):
        for x in range(three, three + 3):
            ylo, yhi = jnp.where(odd, ymate[x], ynext[x]), jnp.where(odd, ynext[x], ymate[x])
            for at, row in ((CSW, SW), (CBN, BN)):
                corners[side, at - CSW + x - three] = jnp.concatenate([ylo[row : row + 4], yhi[row : row + 4]], axis=0)
            if 0 <= x - two < 2:
                for d in range(3):
                    row = VE + 3 * d
                    corners[side, CVE - CSW + 2 * d + x - two] = jnp.concatenate(
                        [ylo[row : row + 3], gap, yhi[row : row + 3], gap], axis=0
                    )
    start_by(is_odd("depth"), fill_corners, mate_out, next_out)
    for copy in fill(mate_out, next_out) + fill_corners(mate_out, next_out):
        copy.wait()


def lift_row(table, hi_row, lo_row):
    found = lax.dot_general(table, lo_table(lo_row), (((1,), (0,)), ((), ())), preferred_element_type=F32)
    wide = jnp.broadcast_to(hi_row, (16, Z))
    acc = jnp.zeros((16, Z), F32)
    for k in range(16):
        acc = jnp.where(wide == float(k), found[16 * k : 16 * k + 16], acc)
    total = acc[0:5] + acc[5:10] + acc[10:15]
    return jnp.concatenate([total, jnp.zeros((3, Z), F32)], axis=0)


def lift_five(first, index):
    tile, lane = lax.shift_right_arithmetic(index, 7), index & 127
    found = [jnp.zeros((8, 128), F32)] * NF
    for t in range(TILES):
        here = tile == t
        for f in range(NF):
            row = jnp.broadcast_to(first[t, f : f + 1, :], (8, 128))
            found[f] = jnp.where(here, jnp.take_along_axis(row, lane, axis=1), found[f])
    return found


def step_kernel(
    first, state, velocity, bins, ymate, ynext, xmate, xnext, new_state_out, near_out, out,
    hi, lo, face_bins, face_lift, table, lifted, p, rows, acc, new_state, near_p, sems
):
    for k in range(16):
        pair = jnp.concatenate([first[2 * k], first[2 * k + 1]], axis=1)
        u, m, l = pieces_of(pair)
        block = jnp.concatenate([u[0:5], m[0:5], l[0:5], jnp.zeros((1, 256), F32)], axis=0)
        table[pl.ds(16 * k, 16), :] = block.astype(BF16)
    tab = table[...]
    time_step = COURANT / (1.0 + jnp.max(first[0, 6:7, :]))
    split_bins(bins, hi, lo)
    odd_y, odd_x = is_odd("box"), is_odd("depth")

    def lower(odd, mate, other):
        return jnp.where(odd, mate, other)

    def upper(odd, mate, other):
        return jnp.where(odd, other, mate)

    for x in range(X):
        face_bins[0, x : x + 1, :] = lower(odd_y, ymate[x, BN + 3 : BN + 4, :], ynext[x, BN + 3 : BN + 4, :]) - 1.0
        face_bins[1, x : x + 1, :] = upper(odd_y, ymate[x, BN : BN + 1, :], ynext[x, BN : BN + 1, :]) - 1.0
    face_bins[2] = lower(odd_x, xmate[BN + 3], xnext[BN + 3]) - 1.0
    face_bins[3] = upper(odd_x, xmate[BN], xnext[BN]) - 1.0

    def lift_some(i, carry):
        planes = [x for x in (2 * i, 2 * i + 1) if x < X - 1]
        for x in planes:
            for y in range(Y):
                eight = lift_row(tab, hi[x, pl.ds(y, 1), :], lo[x, pl.ds(y, 1), :])
                for j in range(3):
                    lifted[x, j, pl.ds(8 * y, 8), :] = eight[:, 128 * j : 128 * j + 128]
        for j in range(3):
            at = slice(128 * j, 128 * j + 128)
            for f, value in enumerate(lift_five(first, face_bins[i, :, at].astype(jnp.int32))):
                face_lift[i, f, :, at] = value
        if i < 3:
            for f, value in enumerate(lift_five(first, bins[X - 1, :, 128 * i : 128 * i + 128])):
                lifted[X - 1, i, pl.ds(f, Y, stride=8), :] = value
        else:
            planes.append(X - 1)
        for x in planes:
            for f in range(NF):
                p[f, x + 1, pl.ds(8, 8), :] = state[f, x] - get_field(lifted, x, f)
        return carry

    for i in range(4):
        lift_some(i, 0)
    for f in range(NF):
        p[f, 0, pl.ds(8, 8), :] = lower(odd_x, xmate[f], xnext[f]) - face_lift[2, f]
        p[f, X + 1, pl.ds(8, 8), :] = upper(odd_x, xmate[f], xnext[f]) - face_lift[3, f]
        for x in range(X):
            mate, other = ymate[x, f : f + 1, :], ynext[x, f : f + 1, :]
            p[f, x + 1, 7:8, :] = lower(odd_y, mate, other) - face_lift[0, f, x : x + 1, :]
            p[f, x + 1, 16:17, :] = upper(odd_y, mate, other) - face_lift[1, f, x : x + 1, :]

    acc[...] = jnp.zeros_like(acc)
    lane = lax.broadcasted_iota(jnp.int32, (Y, Z), 1)
    put_rows(rows, 15, jnp.zeros((Y, Z), F32))

    def advect(x, carry):
        v = [velocity[d, x] for d in range(3)]
        up = [jnp.maximum(c, 0.0) for c in v]
        down = [jnp.minimum(c, 0.0) for c in v]
        for f in range(NF):
            c = p[f, x + 1, pl.ds(8, 8), :]
            before = jnp.where(lane == 0, 0.0, pltpu.roll(c, 1, 1))
            after = jnp.where(lane == Z - 1, 0.0, pltpu.roll(c, Z - 1, 1))
            change = up[0] * (c - p[f, x, pl.ds(8, 8), :]) + down[0] * (p[f, x + 2, pl.ds(8, 8), :] - c)
            change += up[1] * (c - p[f, x + 1, pl.ds(7, 8), :]) + down[1] * (p[f, x + 1, pl.ds(9, 8), :] - c)
            change += up[2] * (c - before) + down[2] * (after - c)
            moved = c - time_step * change
            new_state[f, x] = get_field(lifted, x, f) + moved
            for i, piece in enumerate(pieces_of(moved)):
                put_rows(rows, NF * i + f, piece)
        state_copy(x).start()
        add_bins(acc, rows, hi, lo, x)
        return carry

    def state_copy(x):
        return pltpu.make_async_copy(new_state.at[:, x], new_state_out.at[:, x], sems.at[x])


    for x in range(X + 2):
        total = WEIGHTS[0] * p[0, x]
        for f in range(1, NF):
            total += WEIGHTS[f] * p[f, x]
        near_p[x] = total
    near_copy = pltpu.make_async_copy(near_p, near_out, sems.at[X])
    near_copy.start()
    lax.fori_loop(0, X // 2, lambda i, c: advect(2 * i + 1, advect(2 * i, c)), 0)
    put_sums(out, acc, jnp.zeros((2, 256), F32))
    for x in range(X):
        state_copy(x).wait()
    near_copy.wait()


def weighted_rows(tiles):
    total = jnp.zeros((TILES, 128), F32)
    for f in range(NF):
        total += WEIGHTS[f] * tiles[:, f, :]
    return total


def row_table(total, pieces):
    return jnp.concatenate(pieces_of(total)[:pieces], axis=0).astype(BF16)


def lift_one(tab, b):
    high = jnp.floor(b * (1.0 / 128.0))
    low = b - 128.0 * high
    row = lax.broadcasted_iota(jnp.int32, (TILES, Z), 0).astype(F32)
    row16 = lax.broadcasted_iota(jnp.int32, (16, Z), 0).astype(F32).astype(BF16)
    one, zero = jnp.ones((16, Z), BF16), jnp.zeros((16, Z), BF16)
    wide = jnp.broadcast_to(low, (16, Z)).astype(BF16)
    t = jnp.concatenate([jnp.where(wide == row16 + jnp.asarray(16 * k, BF16), one, zero) for k in range(8)], axis=0)
    found = lax.dot_general(tab, t, (((1,), (0,)), ((), ())), preferred_element_type=F32)
    total = found[0:TILES]
    for i in range(1, tab.shape[0] // TILES):
        total += found[TILES * i : TILES * i + TILES]
    return jnp.sum(jnp.where(jnp.broadcast_to(high, (TILES, Z)) == row, total, 0.0), axis=0, keepdims=True)


def lift_eight(table, b):
    index = b.astype(jnp.int32)
    parts = []
    for j in range(3):
        cut = index[:, 128 * j : 128 * j + 128]
        tile, lane = lax.shift_right_arithmetic(cut, 7), cut & 127
        found = jnp.zeros((8, 128), F32)
        for t in range(TILES):
            row = jnp.broadcast_to(table[t : t + 1, :], (8, 128))
            found = jnp.where(tile == t, jnp.take_along_axis(row, lane, axis=1), found)
        parts.append(found)
    return jnp.concatenate(parts, axis=1)


def reach_rows(far):
    near = {0: range(7, 17), 1: range(8, 16)}
    return {d: [y for y in range(8 - far + d, 16 + far - d) if y not in near.get(d, ())] for d in range(far + 1)}


def ring_kernel(
    first, near_p, shifted, velocity, ymate, ynext, xmate, xnext, q_out, bins_out, p, q, high, v, faces, flat, sems, v_sems, out_sems
):
    def own():
        return [
            pltpu.make_async_copy(near_p, p.at[pl.ds(3, 10)], sems.at[0]),
            pltpu.make_async_copy(shifted, high.at[pl.ds(4, 8), pl.ds(8, 8)], sems.at[1]),
        ]

    def along_y(yhi, ylo):
        return [
            pltpu.make_async_copy(ylo, faces.at[0, pl.ds(0, 8)], sems.at[2]),
            pltpu.make_async_copy(yhi, faces.at[1, pl.ds(0, 8)], sems.at[3]),
        ]

    def along_x(xhi, xlo):
        blocks = [
            (xlo.at[pl.ds(SW, 3)], p.at[pl.ds(0, 3), pl.ds(8, 8)]),
            (xhi.at[pl.ds(SW + 1, 3)], p.at[pl.ds(13, 3), pl.ds(8, 8)]),
            (xlo.at[pl.ds(BN, 4)], high.at[pl.ds(0, 4), pl.ds(8, 8)]),
            (xhi.at[pl.ds(BN, 4)], high.at[pl.ds(12, 4), pl.ds(8, 8)]),
            (xlo.at[pl.ds(CSW, 12)], faces.at[2, pl.ds(0, 12), pl.ds(0, 8)]),
            (xhi.at[pl.ds(CSW, 12)], faces.at[3, pl.ds(0, 12), pl.ds(0, 8)]),
        ]
        return [pltpu.make_async_copy(src, dst, sems.at[4 + i]) for i, (src, dst) in enumerate(blocks)]

    def own_speed():
        return [pltpu.make_async_copy(velocity.at[d], v.at[d, pl.ds(3, 8), pl.ds(8, 8)], v_sems.at[d, 0]) for d in range(3)]

    def speed_x(xhi, xlo):
        copies = []
        for d in range(3):
            for i, (src, at) in enumerate(((xlo, 0), (xhi, 11))):
                src = src.at[pl.ds(VE + 3 * d, 3)]
                copies.append(pltpu.make_async_copy(src, v.at[d, pl.ds(at, 3), pl.ds(8, 8)], v_sems.at[d, 1 + i]))
        return copies

    for copy in own():
        copy.start()
    start_by(is_odd("box"), along_y, ymate, ynext)
    start_by(is_odd("depth"), along_x, xmate, xnext)
    for copy in own_speed():
        copy.start()
    start_by(is_odd("depth"), speed_x, xmate, xnext)
    early = own() + along_y(ymate, ynext) + along_x(xmate, xnext)
    late = own_speed() + speed_x(xmate, xnext)
    flat[...] = weighted_rows(first)
    tab = row_table(flat[...], 3)
    for copy in early:
        copy.wait()
    below, above, left, right = (faces.at[i] for i in range(4))
    p[pl.ds(4, 8), 4:7, :] = below[0:8, SW : SW + 3, :]
    p[pl.ds(4, 8), 17:20, :] = above[0:8, SW + 1 : SW + 4, :]
    high[pl.ds(4, 8), 4:8, :] = below[0:8, BN : BN + 4, :]
    high[pl.ds(4, 8), 16:20, :] = above[0:8, BN : BN + 4, :]
    for dst, corner in ((p, 0), (high, CBN - CSW)):
        for ref, at in ((left, 1), (right, 12)):
            dst[pl.ds(at, 3), 4:8, :] = ref[pl.ds(corner, 3), 0:4, :]
            dst[pl.ds(at, 3), 16:20, :] = ref[pl.ds(corner, 3), 4:8, :]
    bins_copy = pltpu.make_async_copy(high, bins_out, out_sems.at[0])
    bins_copy.start()
    rows = reach_rows(4)

    def lift_x(x, rows, block):
        if block:
            p[x, 8:16, :] = p[x, 8:16, :] - lift_eight(flat, high[x, 8:16, :] - 1.0)
        for y in rows:
            p[x, y : y + 1, :] = p[x, y : y + 1, :] - lift_one(tab, high[x, y : y + 1, :] - 1.0)

    def lift_sides(side, carry):
        for d in range(2, 5):
            lift_x((4 - d) + side * (7 + 2 * d), [y for y in rows[d] if not 8 <= y < 16], True)
        lift_x(3 + side * 9, rows[1], False)
        for i in range(4):
            lift_x(4 + 4 * side + i, rows[0], False)
        return carry

    for side in range(2):
        lift_sides(side, 0)
    for copy in late:
        copy.wait()
    for d in range(3):
        row, corner = VE + 3 * d, CVE - CSW + 2 * d
        v[d, pl.ds(3, 8), 5:8, :] = below[0:8, row : row + 3, :]
        v[d, pl.ds(3, 8), 16:19, :] = above[0:8, row : row + 3, :]
        for ref, at in ((left, 1), (right, 11)):
            v[d, pl.ds(at, 2), 5:8, :] = ref[pl.ds(corner, 2), 0:3, :]
            v[d, pl.ds(at, 2), 16:19, :] = ref[pl.ds(corner, 2), 4:7, :]
    time_step = COURANT / (1.0 + jnp.max(first[0, 6:7, :]))
    lane = lax.broadcasted_iota(jnp.int32, (TALL, Z), 1)

    q_copies = [
        pltpu.make_async_copy(q.at[pl.ds(7 * i, 7)], q_out.at[pl.ds(7 * i, 7)], out_sems.at[1 + i]) for i in range(2)
    ]
    for x in range(14):
        c = p[x + 1]
        sides = (
            (p[x], p[x + 2]),
            (pltpu.roll(c, 1, 0), pltpu.roll(c, TALL - 1, 0)),
            (jnp.where(lane == 0, 0.0, pltpu.roll(c, 1, 1)), jnp.where(lane == Z - 1, 0.0, pltpu.roll(c, Z - 1, 1))),
        )
        change = jnp.zeros((TALL, Z), F32)
        for d, (before, after) in enumerate(sides):
            change += jnp.maximum(v[d, x], 0.0) * (c - before) + jnp.minimum(v[d, x], 0.0) * (after - c)
        q[x] = c - time_step * change
        if x % 7 == 6:
            q_copies[x // 7].start()
    for copy in q_copies:
        copy.wait()
    bins_copy.wait()


def relax_kernel(
    second_in, first_in, q_in, bins_in, potential_out, profile_out, src, high, pot, flat, second, first, potential, profile, sems, out_sems
):
    tables = [
        pltpu.make_async_copy(second_in, second, sems.at[4, 0]),
        pltpu.make_async_copy(first_in, first, sems.at[4, 1]),
    ]
    blocks = []
    for at, n in ((3, 4), (7, 4), (0, 3), (11, 3)):
        bins_at = pl.ds(at + 1, n)
        at = pl.ds(at, n)
        i = len(blocks)
        blocks.append([
            pltpu.make_async_copy(q_in.at[at], src.at[at], sems.at[i, 0]),
            pltpu.make_async_copy(bins_in.at[bins_at], high.at[bins_at], sems.at[i, 1]),
        ])
    for pair in [tables] + blocks:
        for copy in pair:
            copy.start()
    for copy in tables:
        copy.wait()
    for t in range(TILES):
        second[t] = second[t] / jnp.maximum(first[t, 5:6, :], 1.0)
    flat[...] = weighted_rows(second)
    tab = row_table(flat[...], 2)
    for t in range(TILES):
        profile[:, 128 * t : 128 * t + 128] = (first[t] + second[t])[0:NF]
    profile_copy = pltpu.make_async_copy(profile, profile_out, out_sems.at[0])
    profile_copy.start()

    def lift_x(x, rows, block):
        if block:
            src[x, 8:16, :] = src[x, 8:16, :] - lift_eight(flat, high[x + 1, 8:16, :] - 1.0)
        for y in rows:
            src[x, y : y + 1, :] = src[x, y : y + 1, :] - lift_one(tab, high[x + 1, y : y + 1, :] - 1.0)
        scaled = src[x] * (OMEGA_RELAX / DIAGONAL)
        src[x] = scaled
        pot[0, x] = scaled

    def lift_sides(side, carry):
        for d in range(1, 4):
            rows = [y for y in range(5 + d, 19 - d) if d == 3 or not 8 <= y < 16]
            lift_x((3 - d) + side * (7 + 2 * d), rows, d < 3)
        return carry

    for h in range(2):
        for copy in blocks[h]:
            copy.wait()
        for x in range(3 + 4 * h, 7 + 4 * h):
            lift_x(x, (5, 6, 7, 16, 17, 18), True)
    for pair in blocks[2:]:
        for copy in pair:
            copy.wait()
    for side in range(2):
        lift_sides(side, 0)
    lane = lax.broadcasted_iota(jnp.int32, (TALL, Z), 1)
    for s in range(1, 4):
        now, later = (s + 1) % 2, s % 2
        for x in range(s, 14 - s):
            c = pot[now, x]
            near = pot[now, x - 1] + pot[now, x + 1]
            near += pltpu.roll(c, 1, 0) + pltpu.roll(c, TALL - 1, 0)
            near += jnp.where(lane == 0, 0.0, pltpu.roll(c, 1, 1)) + jnp.where(lane == Z - 1, 0.0, pltpu.roll(c, Z - 1, 1))
            new = (1.0 - OMEGA_RELAX) * c + (src[x] + (OMEGA_RELAX / DIAGONAL) * near)
            if s < 3:
                pot[later, x] = jnp.where(high[x + 1] < 0.5, 0.0, new)
            else:
                potential[x - 3] = new[8:16]
    potential_copy = pltpu.make_async_copy(potential, potential_out, out_sems.at[1])
    potential_copy.start()
    potential_copy.wait()
    profile_copy.wait()


def f32_like(*shape):
    return jax.ShapeDtypeStruct(shape, F32)


def call(kernel, plan, *args):
    micros, out_shape, scratch, more = plan
    more = dict(more)
    limit = more.pop("megabytes") * 1024 * 1024
    return pl.pallas_call(
        kernel,
        out_shape=out_shape,
        cost_estimate=pl.CostEstimate(flops=micros * 1_000_000_000, bytes_accessed=0, transcendentals=0),
        scratch_shapes=[pltpu.VMEM(*part) if isinstance(part, tuple) else part for part in scratch],
        compiler_params=pltpu.CompilerParams(vmem_limit_bytes=limit),
        **more,
    )(*args)


def exchange(to_mate, to_next, axis):
    count = lax.axis_size(axis)
    mates = [(i, i ^ 1) for i in range(count)]
    others = [pair for i in range(1, count - 1, 2) for pair in ((i, i + 1), (i + 1, i))]
    return lax.ppermute(to_mate, axis, mates), lax.ppermute(to_next, axis, others)


def added(tiles):
    total, top = tiles[0], tiles[0]
    for i in range(1, tiles.shape[0]):
        total, top = total + tiles[i], jnp.maximum(top, tiles[i])
    return jnp.where(lax.broadcasted_iota(jnp.int32, total.shape, total.ndim - 2) == 6, top, total)


def merge_kernel(tiles, copies):
    total = added(tiles)
    for i in range(copies.shape[0]):
        copies[i] = total


def divide_kernel(tiles, copies):
    total = added(tiles)
    row = lax.broadcasted_iota(jnp.int32, total.shape, 1)
    mean = jnp.where(row < NF, total / jnp.maximum(total[:, 5:6, :], 1.0), total)
    for i in range(MEMBERS):
        copies[i] = mean


def groups_of(varied):
    sizes = (4, 8, 4, 2)
    fixed = [d for d in range(4) if d not in varied]
    places = np.arange(256).reshape(sizes).transpose(fixed + list(varied))
    return places.reshape(-1, math.prod(sizes[d] for d in varied)).tolist()


SHARE_GROUPS = groups_of((0, 2))
OTHER_GROUPS = groups_of((1, 3))
LAYER_GROUPS = groups_of((0, 2, 3))
COLUMN_GROUPS = groups_of((1,))
def swap(parts, groups):
    return lax.all_to_all(parts, ("box", "depth"), 0, 0, axis_index_groups=groups, tiled=True)


def in_members(tiles):
    return tiles.reshape(MEMBERS, TILES // MEMBERS, 8, 128)


VISIBLE = pl.BlockSpec(memory_space=pltpu.VMEM)
REMOTE = pl.BlockSpec(memory_space=pl.ANY)
SUMS = (
    7,
    tuple(pltpu.HBM(shape, F32) for shape in ((X, TALL, Z), (X, TALL, Z), (X, Y, Z), (X, Y, Z), (TILES, 8, 128))),
    [
        ((X, Y, Z), F32), ((X, Y, Z), F32), ((3, Y * 16, 128), F32), ((256, 256), F32),
        ((NF, X, Y, Z), F32), ((3, X, Y, Z), F32), ((X, Y, Z), jnp.int32),
        ((X, TALL, Z), F32), ((X, TALL, Z), F32), ((X, Y, Z), F32), ((X, Y, Z), F32), ((TILES, 8, 128), F32),
        pltpu.SemaphoreType.DMA((5, 2)), pltpu.SemaphoreType.DMA((4, 4)),
    ],
    dict(in_specs=[REMOTE] * 3, out_specs=(REMOTE,) * 5, megabytes=58),
)
PACK_X = (
    2,
    (f32_like(PLANES, Y, Z), f32_like(PLANES, Y, Z)),
    [((2, PLANES - CSW, Y, Z), F32), pltpu.SemaphoreType.DMA((2, 7))],
    dict(in_specs=[REMOTE] * 4 + [VISIBLE] * 2, out_specs=(REMOTE, REMOTE), megabytes=20),
)
STEP = (
    14,
    (f32_like(NF, X, Y, Z), pltpu.HBM((X + 2, TALL, Z), F32), f32_like(TILES, 8, 128)),
    [
        ((X, Y, Z), F32), ((X, Y, Z), F32), ((4, Y, Z), F32), ((4, NF, Y, Z), F32), ((256, 256), BF16),
        ((X, 3, 64, 128), F32), ((NF, X + 2, TALL, Z), F32), ((3, Y * 16, 128), F32), ((256, 256), F32),
        ((NF, X, Y, Z), F32), ((X + 2, TALL, Z), F32), pltpu.SemaphoreType.DMA((X + 1,)),
    ],
    dict(out_specs=(REMOTE, REMOTE, VISIBLE), megabytes=24),
)
RING = (
    8,
    (f32_like(14, TALL, Z), f32_like(16, TALL, Z)),
    [
        ((16, TALL, Z), F32), ((14, TALL, Z), F32), ((16, TALL, Z), F32), ((3, 14, TALL, Z), F32), ((4, 12, TALL, Z), F32), ((TILES, 128), F32),
        pltpu.SemaphoreType.DMA((10,)), pltpu.SemaphoreType.DMA((3, 3)), pltpu.SemaphoreType.DMA((3,)),
    ],
    dict(in_specs=[VISIBLE] + [REMOTE] * 7, out_specs=(REMOTE, REMOTE), megabytes=58),
)
RELAX = (
    9,
    (pltpu.HBM((X, Y, Z), F32), pltpu.HBM((NF, NBINS), F32)),
    [
        ((14, TALL, Z), F32), ((16, TALL, Z), F32), ((2, 14, TALL, Z), F32), ((TILES, 128), F32),
        ((TILES, 8, 128), F32), ((TILES, 8, 128), F32), ((X, Y, Z), F32), ((NF, NBINS), F32),
        pltpu.SemaphoreType.DMA((5, 2)), pltpu.SemaphoreType.DMA((2,)),
    ],
    dict(in_specs=[REMOTE] * 4, out_specs=(REMOTE, REMOTE), megabytes=58),
)


MERGE = (0, f32_like(MEMBERS, 2, 8, 128), [], dict(megabytes=20))
COLUMN = (0, f32_like(8, 8, 128), [], dict(megabytes=20))
LAYER = (0, f32_like(TILES, 8, 128), [], dict(megabytes=20))


def per_device(state, velocity, bins):
    to_mate, to_next, weighted, shifted, tiles = call(sums_kernel, SUMS, state, velocity, bins)
    ymate, ynext = exchange(to_mate, to_next, "box")
    to_mate, to_next = call(pack_x_kernel, PACK_X, state, velocity, weighted, shifted, ymate, ynext)
    xmate, xnext = exchange(to_mate, to_next, "depth")
    copies = call(merge_kernel, MERGE, swap(in_members(tiles), SHARE_GROUPS))
    copies = call(divide_kernel, MERGE, swap(copies, OTHER_GROUPS))
    first = swap(copies, SHARE_GROUPS).reshape(TILES, 8, 128)
    new_state, near_p, tiles = call(step_kernel, STEP, first, state, velocity, bins, ymate, ynext, xmate, xnext)
    q, wide_bins = call(ring_kernel, RING, first, near_p, shifted, velocity, ymate, ynext, xmate, xnext)
    copies = call(merge_kernel, COLUMN, swap(tiles, LAYER_GROUPS))
    copies, q, wide_bins = lax.optimization_barrier((copies, q, wide_bins))
    copies = call(merge_kernel, LAYER, swap(copies, COLUMN_GROUPS))
    second = swap(copies, LAYER_GROUPS)
    potential, profile = call(relax_kernel, RELAX, second, first, q, wide_bins)
    return (new_state, potential, profile)


def solution(mesh):
    return jax.shard_map(
        per_device,
        mesh=mesh,
        in_specs=(
            P(None, "depth", "box", None),
            P(None, "depth", "box", None),
            P("depth", "box", None),
        ),
        out_specs=(P(None, "depth", "box", None), P("depth", "box", None), P()),
        check_vma=False,
    )
```
